32 devices in a mesh: tm: 4 (over z), space: 8 (over y, x, core).
Axes of the slice: x: 2, y: 2, z: 4, core: 2. Of those that a mesh axis runs over, the one named last changes fastest.
Arguments:
- starts: float32 [4, 8, 256, 1024], P('tm', None, 'space'), may hold values from -3 to 3
- diffusivity: bfloat16 [8, 256, 1024], P(None, 'space'), may hold values from 0.25 to 1
- reaction: bfloat16 [8, 256, 1024], P(None, 'space'), may hold values from 0.5 to 2
Outputs:
- next_starts: float32 [4, 8, 256, 1024], P('tm', None, 'space')
The draws below stay inside these ranges and needn't reach their ends.
All inputs are finite; a program needn't handle non-finite values.
Results may differ from the reference program's by a relative error of at most 0.0003.
Values sent between devices are 32-bit elements; how exact they have to be, the bound alone decides.
No kernel may reach another device: no remote copies, remote signals or barrier semaphores. Data moves between devices by JAX's collectives and lax.ppermute only.
A program may use at most 128 MiB of HBM per device.

```python
import math
import jax
import jax.numpy as jnp
from jax import lax

Z = 8
NX = 1024
FINE = 4
COARSE = 2
SLICES = 4
NY = 256


def block_scale(own_key, extent, cuts, least, largest):
    def one(dim, parts):
        steps = jax.random.uniform(jax.random.fold_in(jax.random.fold_in(own_key, 6), dim), (parts,), jnp.float32, least / len(cuts), largest / len(cuts))
        return jnp.repeat(jnp.exp(steps), extent[dim] // parts).reshape((-1,) + (1,) * (len(extent) - dim - 1))

    level = one(*cuts[0])
    for cut in cuts[1:]:
        level = level * one(*cut)
    return level


def normal_values(stream_key, dims, scale, reach, split=(), held_as=jnp.bfloat16):
    level = block_scale(stream_key, dims, split, -0.22, 0.18) if split else 1.0
    entries = jax.random.normal(stream_key, dims, jnp.float32) * scale * level
    return jnp.minimum(jnp.maximum(entries, -reach), reach).astype(held_as)


def setup_inputs(seed: int = 0) -> dict:
    key_of = jax.random.split(jax.random.key(seed), 4)
    starts = normal_values(key_of[0], (SLICES, Z, NY, NX), 0.7, 3.0, ((0, 4), (2, 8)), jnp.float32)
    diffusivity = jnp.clip(jnp.exp(math.log(1.0) - 1.3862944 * jax.random.uniform(key_of[1], (Z, NY, NX), jnp.float32) ** block_scale(key_of[1], (Z, NY, NX), ((1, 8),), -0.2, 0.2)), 0.25, 1.0).astype(jnp.bfloat16)
    reaction = jnp.clip(0.5 + 1.5 * jax.random.uniform(key_of[2], (Z, NY, NX), jnp.float32) ** block_scale(key_of[2], (Z, NY, NX), ((1, 8),), -0.2, 0.2), 0.5, 2.0).astype(jnp.bfloat16)
    return {"starts": starts, "diffusivity": diffusivity, "reaction": reaction}


DT = 0.05
VEL = 0.5


def restrict(values):
    layers, height, breadth = values.shape
    return values.reshape(layers, height // 4, 4, breadth // 4, 4).mean(axis=(2, 4))


def pad_rows(values):
    return jnp.pad(values, ((0, 0), (1, 1), (0, 0)))


def fine_update(values, rowed, diffusion, growth):
    upper_row = rowed[:, 2:, :]
    lower_row = rowed[:, :-2, :]
    z_padded = jnp.pad(values, ((1, 1), (0, 0), (0, 0)))
    x_padded = jnp.pad(values, ((0, 0), (0, 0), (1, 1)))
    z_above = z_padded[2:]
    z_below = z_padded[:-2]
    x_next = x_padded[:, :, 2:]
    x_prev = x_padded[:, :, :-2]
    laplace = z_above + z_below + upper_row + lower_row + x_next + x_prev - 6.0 * values
    drift = VEL * 0.5 * ((upper_row - lower_row) + (x_next - x_prev))
    return values + DT * (diffusion * laplace - drift + growth * (values - values * values * values / 3.0))


def coarse_update(values, rowed, diffusion, growth):
    upper_row = rowed[:, 2:, :]
    lower_row = rowed[:, :-2, :]
    z_padded = jnp.pad(values, ((1, 1), (0, 0), (0, 0)))
    x_padded = jnp.pad(values, ((0, 0), (0, 0), (1, 1)))
    x_next = x_padded[:, :, 2:]
    x_prev = x_padded[:, :, :-2]
    vertical = z_padded[2:] + z_padded[:-2] - 2.0 * values
    level = (upper_row + lower_row + x_next + x_prev - 4.0 * values) / 16.0
    drift = VEL * ((upper_row - lower_row) + (x_next - x_prev)) / 8.0
    return values + 2.0 * DT * (diffusion * (vertical + level) - drift + growth * (values - values * values * values / 3.0))


def reference(starts, diffusivity, reaction):
    diffusion = diffusivity.astype(jnp.float32)
    growth = reaction.astype(jnp.float32)
    coarse_diff = restrict(diffusion)
    coarse_grow = restrict(growth)

    def propagate(values):
        for sweep in range(FINE):
            values = fine_update(values, pad_rows(values), diffusion, growth)
        return values

    def advance(values):
        for sweep in range(COARSE):
            values = coarse_update(values, pad_rows(values), coarse_diff, coarse_grow)
        return values

    fine_end = lax.map(propagate, starts)
    end_coarse = lax.map(restrict, fine_end)
    prior_coarse = lax.map(advance, lax.map(restrict, starts))
    positions = jnp.arange(SLICES, dtype=jnp.int32)
    all_jumps = end_coarse - jnp.where(positions[:, None, None, None] > 0, prior_coarse, 0.0)

    def link_slice(state_now, inputs):
        position, jump_term = inputs
        advanced = jnp.where(position > 0, advance(state_now), 0.0) + jump_term
        return advanced, advanced

    unused, chained = lax.scan(link_slice, jnp.zeros_like(all_jumps[0]), (positions, all_jumps))
    correction = chained - end_coarse
    prolonged = jnp.repeat(jnp.repeat(correction, 4, axis=2), 4, axis=3)
    return fine_end + prolonged
```

```python
import functools

import jax
import jax.numpy as jnp
from jax import lax
from jax.experimental import pallas as pl
from jax.experimental.pallas import tpu as pltpu
from jax.sharding import PartitionSpec as P

FINE = 4
COARSE = 2
DT = 0.05
VEL = 0.5
LANES = 128
F32 = jnp.float32
BF16 = jnp.bfloat16

VMEM = pl.BlockSpec(memory_space=pltpu.VMEM)
ANY = pl.BlockSpec(memory_space=pl.ANY)


def params(mib):
    return pltpu.CompilerParams(vmem_limit_bytes=mib * 2**20)


def struct(*shape):
    return jax.ShapeDtypeStruct(shape, F32)


def parity():
    return lax.rem(lax.axis_index("space"), 2)


def tiles_of(ref, row, breadth):
    return [ref[row, :, i : i + LANES] for i in range(0, breadth, LANES)]


def put_tiles(ref, row, tiles):
    for i, tile in enumerate(tiles):
        ref[row, :, i * LANES : (i + 1) * LANES] = tile


def masks():
    lane = lax.broadcasted_iota(jnp.int32, (8, LANES), 1)
    level = lax.broadcasted_iota(jnp.int32, (8, LANES), 0)
    return lane == 0, lane == LANES - 1, level == 0, level == 7


def neighbours(tiles, edges):
    first, last, bottom, top = edges
    back = [pltpu.roll(t, LANES - 1, 1) for t in tiles]
    forth = [pltpu.roll(t, 1, 1) for t in tiles]
    zero = jnp.zeros_like(tiles[0])
    x_next = [jnp.where(last, b, a) for a, b in zip(back, back[1:] + [zero])]
    x_prev = [jnp.where(first, b, a) for a, b in zip(forth, [zero] + forth[:-1])]
    levels = [
        jnp.where(top, 0.0, pltpu.roll(t, 7, 0)) + jnp.where(bottom, 0.0, pltpu.roll(t, 1, 0))
        for t in tiles
    ]
    return x_next, x_prev, levels


def fine_row(state, row, coef_a, coef_b, coef_k, coef_row, breadth, edges):
    tiles = tiles_of(state, row, breadth)
    x_next, x_prev, levels = neighbours(tiles, edges)
    out = []
    for i, u in enumerate(tiles):
        span = slice(i * LANES, (i + 1) * LANES)
        plus = state[row + 1, :, span] + x_next[i]
        minus = state[row - 1, :, span] + x_prev[i]
        own = u * (coef_a[coef_row, :, span] - coef_b[coef_row, :, span] * (u * u))
        spread = coef_k[coef_row, :, span] * ((plus + minus) + levels[i])
        out.append((own + spread) - (0.5 * VEL * DT) * (plus - minus))
    return out


def coarse_row(state, row, coef_k, coef_g, coef_row, breadth, edges):
    tiles = tiles_of(state, row, breadth)
    x_next, x_prev, levels = neighbours(tiles, edges)
    out = []
    for i, c in enumerate(tiles):
        span = slice(i * LANES, (i + 1) * LANES)
        plus = state[row + 1, :, span] + x_next[i]
        minus = state[row - 1, :, span] + x_prev[i]
        k = coef_k[coef_row, :, span]
        g = coef_g[coef_row, :, span]
        bend = (levels[i] - 2.0 * c) + ((plus + minus) - 4.0 * c) * (1.0 / 16.0)
        drift = (VEL / 8.0) * (plus - minus)
        out.append(c + (2.0 * DT) * (k * bend - drift + g * (c - c * c * c * (1.0 / 3.0))))
    return out


def split_dot(values, matrix):
    high = values.astype(BF16)
    rest = values - high.astype(F32)
    mid = rest.astype(BF16)
    low = (rest - mid.astype(F32)).astype(BF16)
    dot = functools.partial(jnp.dot, preferred_element_type=F32)
    return dot(high, matrix) + (dot(mid, matrix) + dot(low, matrix))


def pool_matrix(breadth, value):
    fine = lax.broadcasted_iota(jnp.int32, (breadth, breadth // 4), 0)
    coarse = lax.broadcasted_iota(jnp.int32, (breadth, breadth // 4), 1)
    return jnp.where(fine // 4 == coarse, value, 0.0).astype(BF16)


def spread_matrix(breadth):
    coarse = lax.broadcasted_iota(jnp.int32, (breadth // 4, breadth), 0)
    fine = lax.broadcasted_iota(jnp.int32, (breadth // 4, breadth), 1)
    return jnp.where(fine // 4 == coarse, 1.0, 0.0).astype(BF16)


def pooled(ref, first_row, coarse_rows, pool):
    sums = []
    for c in range(coarse_rows):
        r = first_row + 4 * c
        sums.append((ref[r] + ref[r + 1]) + (ref[r + 2] + ref[r + 3]))
    return split_dot(jnp.concatenate(sums, axis=0), pool)


def pack_kernel(u_hbm, k_hbm, g_hbm, even_ref, odd_ref, u_nat, k_nat, g_nat, k_wide, g_wide, sems):
    height = u_hbm.shape[2]
    copies = []
    for side, (low, low16) in enumerate(((0, 0), (height - 8, height - 16))):
        copies.append(pltpu.make_async_copy(u_hbm.at[0, :, pl.ds(low, 8), :], u_nat.at[side], sems.at[0, side]))
        copies.append(pltpu.make_async_copy(k_hbm.at[:, pl.ds(low16, 16), :], k_nat.at[side], sems.at[1, side]))
        copies.append(pltpu.make_async_copy(g_hbm.at[:, pl.ds(low16, 16), :], g_nat.at[side], sems.at[2, side]))
    for copy in copies:
        copy.start()
    for copy in copies:
        copy.wait()

    def fill(side, ref):
        k_wide[...] = k_nat[side].astype(F32)
        g_wide[...] = g_nat[side].astype(F32)
        for i in range(4):
            ref[i] = u_nat[side, :, (4 if side else 0) + i, :]
        for i in range(3):
            ref[4 + i] = k_wide[:, (13 if side else 0) + i, :]
            ref[7 + i] = g_wide[:, (13 if side else 0) + i, :]

    even_device = parity() == 0

    @pl.when(even_device)
    def _():
        fill(0, odd_ref)
        fill(1, even_ref)

    @pl.when(jnp.logical_not(even_device))
    def _():
        fill(1, odd_ref)
        fill(0, even_ref)


def pack(starts, diffusivity, reaction):
    breadth = starts.shape[3]
    return pl.pallas_call(
        pack_kernel,
        out_shape=[struct(10, 8, breadth)] * 2,
        in_specs=[ANY] * 3,
        out_specs=[VMEM] * 2,
        scratch_shapes=[
            pltpu.VMEM((2, 8, 8, breadth), F32),
            pltpu.VMEM((2, 8, 16, breadth), BF16),
            pltpu.VMEM((2, 8, 16, breadth), BF16),
            pltpu.VMEM((8, 16, breadth), F32),
            pltpu.VMEM((8, 16, breadth), F32),
            pltpu.SemaphoreType.DMA((3, 2)),
        ],
        compiler_params=params(16),
        name="pack_rows",
    )(starts, diffusivity, reaction)


def set_coefs(k, g, a_ref, b_ref, k_ref, row):
    k = DT * k
    g = DT * g
    k_ref[row] = k
    b_ref[row] = g * (1.0 / 3.0)
    a_ref[row] = 1.0 + (g - 6.0 * k)


def inner_kernel(
    u_hbm, k_hbm, g_hbm, got_ref, fine_ref, edge_ref, coarse_ref, end_ref,
    one, two, coef_a, coef_b, coef_k, k_nat, g_nat, k_wide, g_wide, sems,
):
    height, breadth = u_hbm.shape[2:]
    small = height // 4
    even_side = parity() == 0
    u_copies = [
        pltpu.make_async_copy(u_hbm.at[0, z], one.at[pl.ds(4, height), z, :], sems.at[z]) for z in range(8)
    ]
    k_copy = pltpu.make_async_copy(k_hbm, k_nat, sems.at[8])
    g_copy = pltpu.make_async_copy(g_hbm, g_nat, sems.at[9])
    for copy in [k_copy, g_copy] + u_copies:
        copy.start()
    got = jnp.where(even_side, 4 + height, 0)
    lost = jnp.where(even_side, 0, 4 + height)
    zeros = jnp.zeros((8, breadth), F32)
    for i in range(4):
        one[got + i] = got_ref[i]
        one[lost + i] = zeros
    got_c = jnp.where(even_side, 4 + height, 1)
    lost_c = jnp.where(even_side, 1, 4 + height)
    for i in range(3):
        set_coefs(got_ref[4 + i], got_ref[7 + i], coef_a, coef_b, coef_k, got_c + i)
        coef_a[lost_c + i] = zeros
        coef_b[lost_c + i] = zeros
        coef_k[lost_c + i] = zeros
    pool = pool_matrix(breadth, 1.0 / 16.0)
    k_copy.wait()
    k_wide[...] = k_nat[...].astype(F32)
    g_copy.wait()
    g_wide[...] = g_nat[...].astype(F32)
    sums_k = []
    sums_g = []
    for c in range(small):
        k_rows = [k_wide[:, 4 * c + i, :] for i in range(4)]
        g_rows = [g_wide[:, 4 * c + i, :] for i in range(4)]
        for i in range(4):
            set_coefs(k_rows[i], g_rows[i], coef_a, coef_b, coef_k, 4 + 4 * c + i)
        sums_k.append((k_rows[0] + k_rows[1]) + (k_rows[2] + k_rows[3]))
        sums_g.append((g_rows[0] + g_rows[1]) + (g_rows[2] + g_rows[3]))
    coarse_ref[1] = split_dot(jnp.concatenate(sums_k, axis=0), pool).reshape(small, 8, breadth // 4)
    coarse_ref[2] = split_dot(jnp.concatenate(sums_g, axis=0), pool).reshape(small, 8, breadth // 4)
    for copy in u_copies:
        copy.wait()
    coarse_ref[0] = pooled(one, 4, small, pool).reshape(small, 8, breadth // 4)

    base = jnp.where(even_side, 4, height - 4)
    for i in range(8):
        edge_ref[0, i] = one[base + i]
        edge_ref[1, i] = coef_a[base + i]
        edge_ref[2, i] = coef_b[base + i]
        edge_ref[3, i] = coef_k[base + i]

    edges = masks()

    def sweep(source, target, low, high, shift):
        def body(row, carry):
            put_tiles(target, row - shift, fine_row(source, row, coef_a, coef_b, coef_k, row, breadth, edges))
            return carry

        lax.fori_loop(low, high, body, 0, unroll=2)

    sweep(one, two, 1, height + 7, 0)
    sweep(two, one, 2, height + 6, 0)
    sweep(one, two, 3, height + 5, 0)
    sweep(two, fine_ref, 4, height + 4, 4)
    end_ref[...] = pooled(fine_ref, 0, small, pool).reshape(small, 8, breadth // 4)


def inner(starts, diffusivity, reaction, got):
    height, breadth = starts.shape[2:]
    small = height // 4
    wide = pltpu.VMEM((height + 8, 8, breadth), F32)
    return pl.pallas_call(
        inner_kernel,
        out_shape=[
            struct(height, 8, breadth),
            struct(4, 8, 8, breadth),
            struct(3, small, 8, breadth // 4),
            struct(small, 8, breadth // 4),
        ],
        in_specs=[ANY] * 3 + [VMEM],
        out_specs=[VMEM] * 4,
        scratch_shapes=[wide] * 5
        + [
            pltpu.VMEM((8, height, breadth), BF16),
            pltpu.VMEM((8, height, breadth), BF16),
            pltpu.VMEM((8, height, breadth), F32),
            pltpu.VMEM((8, height, breadth), F32),
            pltpu.SemaphoreType.DMA((10,)),
        ],
        compiler_params=params(24),
        cost_estimate=pl.CostEstimate(flops=30_000_000, bytes_accessed=4_000_000, transcendentals=0),
        name="inner_updates",
    )(starts, diffusivity, reaction, got)


def rows_for(array, low_side, reach):
    start = jnp.where(low_side, 0, array.shape[1] - reach)
    return lax.dynamic_slice_in_dim(array, start, reach, axis=1)


def exchanges(count):
    even = [(i, i ^ 1) for i in range(count)]
    odd = [(i, (i - 1 if i % 2 == 0 else i + 1) % count) for i in range(count)]
    return even, odd


def alive():
    place = lax.axis_index("space")
    last = lax.axis_size("space") - 1
    return jnp.where(jnp.logical_or(place == 0, place == last), 0.0, 1.0).astype(F32)


def edge_kernel(
    edge_ref, got_ref, end_in, coarse_ref, even_c, odd_c, rows_ref, end_ref, jump_ref,
    one, two, coef_a, coef_b, coef_k, seen, half, coarse_k, coarse_g,
):
    breadth = edge_ref.shape[3]
    small = end_ref.shape[0]
    low_side = parity() == 0
    live = alive()
    edges = masks()
    own_u = jnp.where(low_side, 4, 0)
    own_c = jnp.where(low_side, 4, 0)
    got_u = jnp.where(low_side, 0, 8)
    got_c = jnp.where(low_side, 1, 8)
    for i in range(8):
        one[own_u + i] = edge_ref[0, i]
        coef_a[own_c + i] = edge_ref[1, i]
        coef_b[own_c + i] = edge_ref[2, i]
        coef_k[own_c + i] = edge_ref[3, i]
    for i in range(4):
        one[got_u + i] = got_ref[i] * live
    for i in range(3):
        set_coefs(got_ref[4 + i], got_ref[7 + i], coef_a, coef_b, coef_k, got_c + i)

    def sweep(source, target, low, high, shift):
        def body(row, carry):
            outside = jnp.where(low_side, row < 4, row >= 8)
            factor = jnp.where(outside, live, 1.0)
            tiles = fine_row(source, row, coef_a, coef_b, coef_k, row, breadth, edges)
            put_tiles(target, row - shift, [t * factor for t in tiles])
            return carry

        lax.fori_loop(low, high, body, 0, unroll=2)

    sweep(one, two, 1, 11, 0)
    sweep(two, one, 2, 10, 0)
    sweep(one, two, 3, 9, 0)
    sweep(two, rows_ref, 4, 8, 4)
    pool = pool_matrix(breadth, 1.0 / 16.0)
    end_ref[...] = end_in[...]
    end_ref[jnp.where(low_side, 0, small - 1)] = pooled(rows_ref, 0, 1, pool)

    fill_coarse(seen, coarse_ref.at[0], even_c.at[0], odd_c.at[0], 2, low_side, live)
    fill_coarse(coarse_k, coarse_ref.at[1], even_c.at[1], odd_c.at[1], 2, low_side, live)
    fill_coarse(coarse_g, coarse_ref.at[2], even_c.at[2], odd_c.at[2], 2, low_side, live)
    coarse_sweep(seen, half, coarse_k, coarse_g, 1, small + 3, 2, small, low_side, live, edges)
    first = lax.axis_index("tm") == 0
    for r in range(small):
        tiles = coarse_row(half, 2 + r, coarse_k, coarse_g, 2 + r, breadth // 4, edges)
        for i, tile in enumerate(tiles):
            span = slice(i * LANES, (i + 1) * LANES)
            jump_ref[r, :, span] = end_ref[r, :, span] - jnp.where(first, 0.0, tile)


def fill_coarse(wide, own, even_part, odd_part, reach, low_side, live):
    rows = own.shape[0]
    count = even_part.shape[0]
    for r in range(rows):
        wide[reach + r] = own[r]
    odd_at = jnp.where(low_side, 0, reach + rows)
    even_at = jnp.where(low_side, reach + rows, 0)
    odd_from = jnp.where(low_side, count - reach, 0)
    even_from = jnp.where(low_side, 0, count - reach)
    for i in range(reach):
        wide[odd_at + i] = odd_part[odd_from + i] * live
        wide[even_at + i] = even_part[even_from + i]


def coarse_sweep(source, target, coef_k, coef_g, low, high, reach, rows, low_side, live, edges, shift=0):
    breadth = source.shape[2]
    for row in range(low, high):
        tiles = coarse_row(source, row, coef_k, coef_g, row + shift, breadth, edges)
        if row < reach:
            factor = jnp.where(low_side, live, 1.0)
            tiles = [t * factor for t in tiles]
        elif row >= reach + rows:
            factor = jnp.where(low_side, 1.0, live)
            tiles = [t * factor for t in tiles]
        put_tiles(target, row, tiles)


def edge(edge_rows, got, end, coarse, even_c, odd_c):
    breadth = edge_rows.shape[3]
    small = end.shape[0]
    wide = pltpu.VMEM((12, 8, breadth), F32)
    thin = pltpu.VMEM((small + 4, 8, breadth // 4), F32)
    return pl.pallas_call(
        edge_kernel,
        out_shape=[
            struct(4, 8, breadth),
            struct(small, 8, breadth // 4),
            struct(small, 8, breadth // 4),
        ],
        in_specs=[VMEM] * 6,
        out_specs=[VMEM] * 3,
        scratch_shapes=[wide] * 5 + [thin] * 4,
        compiler_params=params(16),
        name="edge_updates",
    )(edge_rows, got, end, coarse, even_c, odd_c)


def last_kernel(
    fine_hbm, rows_ref, end_ref, jump_ref, before_ref, even_j, odd_j, coarse_ref, even_c, odd_c, out_ref,
    fine_ref, one, two, coarse_k, coarse_g, added, sem,
):
    behind = before_ref.shape[0]
    reach = COARSE * behind
    height, _, breadth = fine_hbm.shape
    small = height // 4
    fetch = pltpu.make_async_copy(fine_hbm, fine_ref, sem.at[0])
    fetch.start()
    low_side = parity() == 0
    live = alive()
    edges = masks()
    slice_id = lax.axis_index("tm")
    fill_coarse(coarse_k, coarse_ref.at[1], even_c.at[1], odd_c.at[1], reach, low_side, live)
    fill_coarse(coarse_g, coarse_ref.at[2], even_c.at[2], odd_c.at[2], reach, low_side, live)
    at = 0
    for j in range(behind):
        width = reach - COARSE * j
        ok = jnp.where(slice_id >= behind - j, 1.0, 0.0).astype(F32)
        target = one if j == 0 else added
        base = reach - width
        for r in range(small):
            target[reach + r] = before_ref[j, r] * ok
        odd_at = jnp.where(low_side, base, reach + small)
        even_at = jnp.where(low_side, reach + small, base)
        for i in range(width):
            target[odd_at + i] = odd_j[at + i] * (ok * live)
            target[even_at + i] = even_j[at + i] * ok
        at += width
        if j > 0:
            for r in range(base, reach + small + width):
                one[r] = one[r] + added[r]
        coarse_sweep(one, two, coarse_k, coarse_g, base + 1, reach + small + width - 1, reach, small, low_side, live, edges)
        coarse_sweep(two, one, coarse_k, coarse_g, base + 2, reach + small + width - 2, reach, small, low_side, live, edges)
    spread = spread_matrix(breadth)
    change = jnp.concatenate(
        [(one[reach + r] + jump_ref[r]) - end_ref[r] for r in range(small)], axis=0
    )
    moved = split_dot(change, spread)
    fetch.wait()
    fixed = jnp.where(low_side, 0, height - 4)
    for i in range(4):
        fine_ref[fixed + i] = rows_ref[i]
    for y in range(height):
        c = y // 4
        out_ref[0, :, y, :] = fine_ref[y] + moved[8 * c : 8 * c + 8]


def last(fine, rows, end, jump, before, even_j, odd_j, coarse, even_c, odd_c):
    height, _, breadth = fine.shape
    small = height // 4
    reach = COARSE * before.shape[0]
    thin = pltpu.VMEM((small + 2 * reach, 8, breadth // 4), F32)
    return pl.pallas_call(
        last_kernel,
        out_shape=struct(1, 8, height, breadth),
        in_specs=[ANY] + [VMEM] * 9,
        out_specs=VMEM,
        scratch_shapes=[pltpu.VMEM((height, 8, breadth), F32)] + [thin] * 5 + [pltpu.SemaphoreType.DMA((1,))],
        compiler_params=params(16),
        name="chain_and_spread",
    )(fine, rows, end, jump, before, even_j, odd_j, coarse, even_c, odd_c)


def relay(jump, coarse, even_c, odd_c, even, odd):
    low_side = parity() == 0
    live = alive()
    small = jump.shape[0]

    def widened(own, even_part, odd_part):
        even_part, odd_part = even_part[:, -2:], odd_part[:, -2:] * live
        low = jnp.where(low_side, odd_part, even_part)
        high = jnp.where(low_side, even_part, odd_part)
        return jnp.concatenate([low, own, high], axis=1)

    def update(values, k, g):
        rows = values.shape[0] - 2
        middle = values[1:-1]
        plus = values[2:] + jnp.pad(middle, ((0, 0), (0, 0), (0, 1)))[:, :, 1:]
        minus = values[:-2] + jnp.pad(middle, ((0, 0), (0, 0), (1, 0)))[:, :, :-1]
        levels = jnp.pad(middle, ((0, 0), (0, 1), (0, 0)))[:, 1:] + jnp.pad(middle, ((0, 0), (1, 0), (0, 0)))[:, :-1]
        bend = levels - 2.0 * middle + (plus + minus - 4.0 * middle) / 16.0
        drift = VEL * (plus - minus) / 8.0
        return middle + 2.0 * DT * (k * bend - drift + g * (middle - middle * middle * middle / 3.0))

    side_e = coarse_halo(coarse, even_c, 2, jnp.logical_not(low_side))
    side_o = coarse_halo(coarse, odd_c, 2, low_side)
    coefs = widened(coarse, side_e, side_o)
    place = lax.axis_index("space")
    start = jnp.where(place == 0, 1, 0)
    stop = jnp.where(place == lax.axis_size("space") - 1, small + 1, small + 2)
    row = jnp.arange(small + 2)[:, None, None]
    inside = jnp.logical_and(row >= start, row < stop)

    def advance(values):
        block = values[None]
        even_v = lax.ppermute(rows_for(block, jnp.logical_not(low_side), 2), "space", even)
        odd_v = lax.ppermute(rows_for(block, low_side, 2), "space", odd)
        wide = widened(block, even_v, odd_v)[0]
        wide = jnp.where(inside, update(wide, coefs[1, 1:-1], coefs[2, 1:-1]), 0.0)
        return update(wide, coarse[1], coarse[2])

    slice_id = lax.axis_index("tm")
    slices = lax.axis_size("tm")
    onward = [(i, i + 1) for i in range(slices - 1)]

    def link(position, state):
        incoming = lax.ppermute(state, "tm", onward)
        return jnp.where(slice_id > 0, advance(incoming), 0.0) + jump

    return lax.fori_loop(0, slices - 1, link, jump)


def coarse_halo(coarse, part, reach, low_side):
    start = jnp.where(low_side, part.shape[1] - reach, 0)
    return lax.dynamic_slice_in_dim(part, start, reach, axis=1)


def per_device(starts, diffusivity, reaction):
    height, breadth = starts.shape[2:]
    small = height // 4
    slices = lax.axis_size("tm")
    behind = slices - 1
    reach = COARSE * behind
    at_once = 0 < behind and reach <= small
    even, odd = exchanges(lax.axis_size("space"))
    low_side = parity() == 0
    high_side = jnp.logical_not(low_side)

    even_rows, odd_rows = pack(starts, diffusivity, reaction)
    odd_got = lax.ppermute(odd_rows, "space", odd)
    even_got = lax.ppermute(even_rows, "space", even)
    fine, edge_rows, coarse, end = inner(starts, diffusivity, reaction, even_got)
    width = reach if at_once else COARSE
    odd_c = lax.ppermute(rows_for(coarse, low_side, width), "space", odd)
    even_c = lax.ppermute(rows_for(coarse, high_side, width), "space", even)
    rows, end, jump = edge(edge_rows, odd_got, end, coarse, even_c, odd_c)
    if at_once:
        before = [
            lax.ppermute(jump, "tm", [(i, (i + k) % slices) for i in range(slices)])
            for k in range(behind, 0, -1)
        ]
        before = jnp.stack(before)

        def outer(low):
            return jnp.concatenate(
                [rows_for(before[j][None], low, reach - COARSE * j)[0] for j in range(behind)], axis=0
            )

        odd_j = lax.ppermute(outer(low_side), "space", odd)
        even_j = lax.ppermute(outer(high_side), "space", even)
        return last(fine, rows, end, jump, before, even_j, odd_j, coarse, even_c, odd_c)
    chained = relay(jump, coarse, even_c, odd_c, even, odd)
    change = jnp.repeat(jnp.repeat(chained - end, 4, axis=0), 4, axis=2)
    fixed = jnp.where(low_side, 0, height - 4)
    fine = lax.dynamic_update_slice_in_dim(fine, rows, fixed, axis=0)
    return jnp.transpose(fine + change, (1, 0, 2))[None]


def solution(mesh):
    in_specs = (P("tm", None, "space", None), P(None, "space", None), P(None, "space", None))
    out_specs = P("tm", None, "space", None)
    return jax.shard_map(per_device, mesh=mesh, in_specs=in_specs, out_specs=out_specs, check_vma=False)
```

```python
import functools

import jax
import jax.numpy as jnp
from jax import lax
from jax.experimental import pallas as pl
from jax.experimental.pallas import tpu as pltpu
from jax.sharding import PartitionSpec as P

FINE = 4
COARSE = 2
DT = 0.05
VEL = 0.5
LANES = 128
F32 = jnp.float32
BF16 = jnp.bfloat16

VMEM = pl.BlockSpec(memory_space=pltpu.VMEM)
ANY = pl.BlockSpec(memory_space=pl.ANY)
HBM = pl.BlockSpec(memory_space=pltpu.HBM)


def params(mib):
    return pltpu.CompilerParams(vmem_limit_bytes=mib * 2**20)


def struct(*shape):
    return jax.ShapeDtypeStruct(shape, F32)


def parity():
    return lax.rem(lax.axis_index("space"), 2)


def tiles_of(ref, row, breadth):
    return [ref[row, :, i : i + LANES] for i in range(0, breadth, LANES)]


def put_tiles(ref, row, tiles):
    for i, tile in enumerate(tiles):
        ref[row, :, i * LANES : (i + 1) * LANES] = tile


def masks():
    lane = lax.broadcasted_iota(jnp.int32, (8, LANES), 1)
    level = lax.broadcasted_iota(jnp.int32, (8, LANES), 0)
    return lane == 0, lane == LANES - 1, level == 0, level == 7


def neighbours(tiles, edges):
    first, last, bottom, top = edges
    back = [pltpu.roll(t, LANES - 1, 1) for t in tiles]
    forth = [pltpu.roll(t, 1, 1) for t in tiles]
    zero = jnp.zeros_like(tiles[0])
    x_next = [jnp.where(last, b, a) for a, b in zip(back, back[1:] + [zero])]
    x_prev = [jnp.where(first, b, a) for a, b in zip(forth, [zero] + forth[:-1])]
    levels = [
        jnp.where(top, 0.0, pltpu.roll(t, 7, 0)) + jnp.where(bottom, 0.0, pltpu.roll(t, 1, 0))
        for t in tiles
    ]
    return x_next, x_prev, levels


def fine_row(state, row, coef_a, coef_b, coef_k, coef_row, breadth, edges):
    tiles = tiles_of(state, row, breadth)
    x_next, x_prev, levels = neighbours(tiles, edges)
    out = []
    for i, u in enumerate(tiles):
        span = slice(i * LANES, (i + 1) * LANES)
        plus = state[row + 1, :, span] + x_next[i]
        minus = state[row - 1, :, span] + x_prev[i]
        own = u * (coef_a[coef_row, :, span] - coef_b[coef_row, :, span] * (u * u))
        spread = coef_k[coef_row, :, span] * ((plus + minus) + levels[i])
        out.append((own + spread) - (0.5 * VEL * DT) * (plus - minus))
    return out


def coarse_row(state, row, coef_k, coef_g, coef_row, breadth, edges):
    tiles = tiles_of(state, row, breadth)
    x_next, x_prev, levels = neighbours(tiles, edges)
    out = []
    for i, c in enumerate(tiles):
        span = slice(i * LANES, (i + 1) * LANES)
        plus = state[row + 1, :, span] + x_next[i]
        minus = state[row - 1, :, span] + x_prev[i]
        k = coef_k[coef_row, :, span]
        g = coef_g[coef_row, :, span]
        bend = (levels[i] - 2.0 * c) + ((plus + minus) - 4.0 * c) * (1.0 / 16.0)
        drift = (2.0 * DT * VEL / 8.0) * (plus - minus)
        out.append(c + ((k * bend - drift) + g * (c - c * c * c * (1.0 / 3.0))))
    return out


def split_dot(values, matrix):
    high = values.astype(BF16)
    rest = values - high.astype(F32)
    mid = rest.astype(BF16)
    low = (rest - mid.astype(F32)).astype(BF16)
    dot = functools.partial(jnp.dot, preferred_element_type=F32)
    return dot(high, matrix) + (dot(mid, matrix) + dot(low, matrix))


def pool_matrix(breadth, value):
    fine = lax.broadcasted_iota(jnp.int32, (breadth, breadth // 4), 0)
    coarse = lax.broadcasted_iota(jnp.int32, (breadth, breadth // 4), 1)
    return jnp.where(fine // 4 == coarse, value, 0.0).astype(BF16)


def spread_matrix(breadth):
    coarse = lax.broadcasted_iota(jnp.int32, (breadth // 4, breadth), 0)
    fine = lax.broadcasted_iota(jnp.int32, (breadth // 4, breadth), 1)
    return jnp.where(fine // 4 == coarse, 1.0, 0.0).astype(BF16)


def pooled(ref, first_row, coarse_rows, pool):
    sums = []
    for c in range(coarse_rows):
        r = first_row + 4 * c
        sums.append((ref[r] + ref[r + 1]) + (ref[r + 2] + ref[r + 3]))
    return split_dot(jnp.concatenate(sums, axis=0), pool)


def set_coefs(k, g, a_ref, b_ref, k_ref, row):
    k = DT * k
    g = DT * g
    k_ref[row] = k
    b_ref[row] = g * (1.0 / 3.0)
    a_ref[row] = 1.0 + (g - 6.0 * k)


def pack_kernel(u_hbm, k_hbm, g_hbm, even_ref, odd_ref, u_nat, k_nat, g_nat, k_wide, g_wide, sems):
    height, breadth = u_hbm.shape[2:]
    copies = []
    for side, (low, low16) in enumerate(((0, 0), (height - 8, height - 16))):
        copies.append(pltpu.make_async_copy(u_hbm.at[0, :, pl.ds(low, 8), :], u_nat.at[side], sems.at[0, side]))
        copies.append(pltpu.make_async_copy(k_hbm.at[:, pl.ds(low16, 16), :], k_nat.at[side], sems.at[1, side]))
        copies.append(pltpu.make_async_copy(g_hbm.at[:, pl.ds(low16, 16), :], g_nat.at[side], sems.at[2, side]))
    for copy in copies:
        copy.start()
    pool = pool_matrix(breadth, 1.0 / 16.0)
    for copy in copies:
        copy.wait()

    def fill(side, ref):
        k_wide[side] = k_nat[side].astype(F32)
        g_wide[side] = g_nat[side].astype(F32)
        u_rows = [u_nat[side, :, i, :] for i in range(8)]
        low = 12 if side else 0
        k_rows = [k_wide[side, :, low + i, :] for i in range(4)]
        g_rows = [g_wide[side, :, low + i, :] for i in range(4)]
        for i in range(4):
            ref[i] = u_rows[(4 if side else 0) + i]
        for i in range(3):
            ref[4 + i] = k_rows[(1 if side else 0) + i]
            ref[7 + i] = g_rows[(1 if side else 0) + i]
        return [(r[0] + r[1]) + (r[2] + r[3]) for r in (u_rows[:4], u_rows[4:], k_rows, g_rows)]

    def both(first, second):
        sums = fill(first, odd_ref) + fill(second, even_ref)
        small = split_dot(jnp.concatenate(sums, axis=0), pool)
        for j, ref in enumerate((odd_ref, even_ref)):
            for i in range(4):
                scale = 1.0 if i < 2 else 2.0 * DT
                row = small[32 * j + 8 * i : 32 * j + 8 * i + 8]
                ref[10, :, i * (breadth // 4) : (i + 1) * (breadth // 4)] = row * scale

    even_device = parity() == 0

    @pl.when(even_device)
    def _():
        both(0, 1)

    @pl.when(jnp.logical_not(even_device))
    def _():
        both(1, 0)


def pack(starts, diffusivity, reaction):
    breadth = starts.shape[3]
    return pl.pallas_call(
        pack_kernel,
        out_shape=[struct(11, 8, breadth)] * 2,
        in_specs=[HBM] * 3,
        out_specs=[VMEM] * 2,
        scratch_shapes=[
            pltpu.VMEM((2, 8, 8, breadth), F32),
            pltpu.VMEM((2, 8, 16, breadth), BF16),
            pltpu.VMEM((2, 8, 16, breadth), BF16),
            pltpu.VMEM((2, 8, 16, breadth), F32),
            pltpu.VMEM((2, 8, 16, breadth), F32),
            pltpu.SemaphoreType.DMA((3, 2)),
        ],
        compiler_params=params(16),
        name="pack_rows",
    )(starts, diffusivity, reaction)


def inner_kernel(
    u_hbm, k_hbm, g_hbm, got_ref, fine_ref, steps_ref, coefs_ref, coarse_ref, end_ref,
    one, two, coef_a, coef_b, coef_k, k_nat, g_nat, flat, sems,
):
    height, breadth = u_hbm.shape[2:]
    columns = breadth // LANES
    small = height // 4
    thin = breadth // 4
    spans = [slice(x * LANES, (x + 1) * LANES) for x in range(columns)]
    above = parity() == 0
    own = pl.multiple_of(jnp.where(above, 0, 8), 8)
    copies = [
        pltpu.make_async_copy(
            u_hbm.at[0, :, :, pl.ds(x * LANES, LANES)], one.at[pl.ds(1, 8), x, pl.ds(8 + own, height), :], sems.at[x]
        )
        for x in range(columns)
    ]
    k_copy = pltpu.make_async_copy(k_hbm, k_nat, sems.at[columns])
    g_copy = pltpu.make_async_copy(g_hbm, g_nat, sems.at[columns + 1])
    for copy in [k_copy, g_copy] + copies:
        copy.start()
    blank = jnp.zeros((8, LANES), F32)
    top = height + 16

    def clear(z, carry):
        for ref in (one, two):
            for x in range(columns):
                ref[z, x, 0:8, :] = blank
                ref[z, x, top : top + 8, :] = blank
        return carry

    lax.fori_loop(0, 10, clear, 0)
    for ref in (one, two):
        for z in (0, 9):
            for x in range(columns):
                ref[z, x, 8:top, :] = jnp.zeros((height + 8, LANES), F32)

    def place(u_row, c_row, tile):
        for x in range(columns):
            for z in range(8):
                one[1 + z, x, 8 + tile : 16 + tile, :] = blank
                coef_a[z, x, tile : tile + 8, :] = blank
                coef_b[z, x, tile : tile + 8, :] = blank
                coef_k[z, x, tile : tile + 8, :] = blank
        for x, span in enumerate(spans):
            for i in range(4):
                one[1:9, x, u_row + i, :] = got_ref[i, :, span]
            for i in range(3):
                k = DT * got_ref[4 + i, :, span]
                g = DT * got_ref[7 + i, :, span]
                coef_k[:, x, c_row + i, :] = k
                coef_b[:, x, c_row + i, :] = g * (1.0 / 3.0)
                coef_a[:, x, c_row + i, :] = 1.0 + (g - 6.0 * k)

    @pl.when(above)
    def _():
        place(8 + height, height, height)

    @pl.when(jnp.logical_not(above))
    def _():
        place(12, 5, 0)

    k_copy.wait()
    g_copy.wait()

    def widen(z, carry):
        for x, span in enumerate(spans):
            for r in range(0, height, 16):
                k = DT * k_nat[z, r : r + 16, span].astype(F32)
                g = DT * g_nat[z, r : r + 16, span].astype(F32)
                rows = pl.ds(own + r, 16)
                coef_k[z, x, rows, :] = k
                coef_b[z, x, rows, :] = g * (1.0 / 3.0)
                coef_a[z, x, rows, :] = 1.0 + (g - 6.0 * k)
        return carry

    lax.fori_loop(0, 8, widen, 0)
    for copy in copies:
        copy.wait()

    lane = lax.broadcasted_iota(jnp.int32, (8, LANES), 1)
    first, final = lane == 0, lane == LANES - 1

    def sweep(source, target, level, shift):
        def body(z, carry):
            for row in range(8, top, 8):
                tiles = [source[z + 1, x, row : row + 8, :] for x in range(columns)]
                back = [pltpu.roll(t, LANES - 1, 1) for t in tiles] + [blank]
                forth = [blank] + [pltpu.roll(t, 1, 1) for t in tiles]
                for x, u in enumerate(tiles):
                    x_next = jnp.where(final, back[x + 1], back[x])
                    x_prev = jnp.where(first, forth[x], forth[x + 1])
                    plus = source[z + 1, x, row + 1 : row + 9, :] + x_next
                    minus = source[z + 1, x, row - 1 : row + 7, :] + x_prev
                    levels = source[z, x, row : row + 8, :] + source[z + 2, x, row : row + 8, :]
                    rows = slice(row - 8, row)
                    own_part = u * (coef_a[z, x, rows, :] - coef_b[z, x, rows, :] * (u * u))
                    spread = coef_k[z, x, rows, :] * ((plus + minus) + levels)
                    out = (own_part + spread) - (0.5 * VEL * DT) * (plus - minus)
                    if shift is None:
                        target[z + level, x, row : row + 8, :] = out
                    else:
                        target[z + level, x, pl.ds(pl.multiple_of(row + shift, 8), 8), :] = out
            return carry

        lax.fori_loop(0, 8, body, 0, unroll=2)

    def keep(step, source):
        def write(row):
            for x, span in enumerate(spans):
                for i in range(2):
                    steps_ref[2 * step + i, :, span] = source[1:9, x, row + i, :]

        @pl.when(above)
        def _():
            write(8 + step)

        @pl.when(jnp.logical_not(above))
        def _():
            write(16 + height - 2 - step)

    def keep_coefs(row):
        for x, span in enumerate(spans):
            for i in range(4):
                coefs_ref[0, i, :, span] = coef_a[:, x, row + i, :]
                coefs_ref[1, i, :, span] = coef_b[:, x, row + i, :]
                coefs_ref[2, i, :, span] = coef_k[:, x, row + i, :]

    @pl.when(above)
    def _():
        keep_coefs(0)

    @pl.when(jnp.logical_not(above))
    def _():
        keep_coefs(8 + height - 4)

    pool = pool_matrix(breadth, 1.0 / 16.0)

    def sums_of(ref, level, start):
        def body(z, carry):
            for x, span in enumerate(spans):
                parts = [ref[z + level, x, pl.ds(start + i, small, stride=4), :] for i in range(4)]
                flat[z, :, span] = (parts[0] + parts[1]) + (parts[2] + parts[3])
            return carry

        lax.fori_loop(0, 8, body, 0)

    def pooled_into(ref, level, start, target, scale):
        sums_of(ref, level, start)
        mean = split_dot(flat[...].reshape(8 * small, breadth), pool) * scale
        flat[:, :, 0:thin] = mean.reshape(8, small, thin)
        for r in range(small):
            target[r] = flat[:, r, 0:thin]

    pooled_into(one, 1, 8 + own, coarse_ref.at[0], 1.0)
    pooled_into(coef_k, 0, own, coarse_ref.at[1], 2.0)
    pooled_into(coef_b, 0, own, coarse_ref.at[2], 6.0)
    keep(0, one)
    sweep(one, two, 1, None)
    keep(1, two)
    sweep(two, one, 1, None)
    keep(2, one)
    sweep(one, two, 1, None)
    keep(3, two)
    sweep(two, fine_ref, 0, jnp.where(above, 0, -8))
    pooled_into(fine_ref, 0, 8, end_ref, 1.0)


def inner(starts, diffusivity, reaction, got):
    height, breadth = starts.shape[2:]
    small = height // 4
    columns = breadth // LANES
    wide = pltpu.VMEM((10, columns, height + 24, LANES), F32)
    coef = pltpu.VMEM((8, columns, height + 8, LANES), F32)
    return pl.pallas_call(
        inner_kernel,
        out_shape=[
            struct(8, columns, height + 16, LANES),
            struct(8, 8, breadth),
            struct(3, 4, 8, breadth),
            struct(3, small, 8, breadth // 4),
            struct(small, 8, breadth // 4),
        ],
        in_specs=[ANY] * 3 + [VMEM],
        out_specs=[VMEM] * 5,
        scratch_shapes=[wide, wide, coef, coef, coef]
        + [
            pltpu.VMEM((8, height, breadth), BF16),
            pltpu.VMEM((8, height, breadth), BF16),
            pltpu.VMEM((8, small, breadth), F32),
            pltpu.SemaphoreType.DMA((columns + 2,)),
        ],
        compiler_params=params(28),
        cost_estimate=pl.CostEstimate(flops=30_000_000, bytes_accessed=4_000_000, transcendentals=0),
        name="inner_updates",
    )(starts, diffusivity, reaction, got)


def rows_for(array, low_side, reach):
    start = jnp.where(low_side, 0, array.shape[1] - reach)
    return lax.dynamic_slice_in_dim(array, start, reach, axis=1)


def exchanges(count):
    even = [(i, i ^ 1) for i in range(count)]
    odd = [(i, (i - 1 if i % 2 == 0 else i + 1) % count) for i in range(count)]
    return even, odd


def alive():
    place = lax.axis_index("space")
    last = lax.axis_size("space") - 1
    return jnp.where(jnp.logical_or(place == 0, place == last), 0.0, 1.0).astype(F32)


def edge_kernel(
    steps_ref, coefs_ref, got_ref, even_ref, end_in, coarse_ref, rows_ref, end_ref, jump_ref,
    zero, one, two, three, coef_a, coef_b, coef_k, seen, half, coarse_k, coarse_g,
):
    breadth = got_ref.shape[2]
    small = end_ref.shape[0]
    low_side = parity() == 0
    live = alive()
    edges = masks()
    states = (zero, one, two, three, rows_ref)
    got_u = jnp.where(low_side, 0, 8)
    got_c = jnp.where(low_side, 1, 8)
    for i in range(4):
        zero[got_u + i] = got_ref[i] * live
        coef_a[4 + i] = coefs_ref[0, i]
        coef_b[4 + i] = coefs_ref[1, i]
        coef_k[4 + i] = coefs_ref[2, i]
    for i in range(3):
        set_coefs(got_ref[4 + i], got_ref[7 + i], coef_a, coef_b, coef_k, got_c + i)
    for step in range(4):
        at = jnp.where(low_side, 4 + step, 6 - step)
        for i in range(2):
            states[step][at + i] = steps_ref[2 * step + i]
    for step in range(1, 5):
        at = jnp.where(low_side, step, 8 - step)
        for i in range(4):
            tiles = fine_row(states[step - 1], at + i, coef_a, coef_b, coef_k, at + i, breadth, edges)
            outside = jnp.logical_or(
                jnp.logical_and(low_side, i < 4 - step), jnp.logical_and(jnp.logical_not(low_side), i >= step)
            )
            if step < 4:
                factor = jnp.where(outside, live, 1.0)
                put_tiles(states[step], at + i, [t * factor for t in tiles])
            else:
                put_tiles(rows_ref, i, tiles)
    pool = pool_matrix(breadth, 1.0 / 16.0)
    end_ref[...] = end_in[...]
    end_ref[jnp.where(low_side, 0, small - 1)] = pooled(rows_ref, 0, 1, pool)

    thin = breadth // 4
    odd_at = jnp.where(low_side, 0, 2 + small)
    even_at = jnp.where(low_side, 2 + small, 0)
    near = jnp.where(low_side, 1, 2 + small)
    far = jnp.where(low_side, 2 + small, 1)
    for r in range(small):
        seen[2 + r] = coarse_ref[0, r]
        coarse_k[2 + r] = coarse_ref[1, r]
        coarse_g[2 + r] = coarse_ref[2, r]
    for i in range(2):
        span = slice(i * thin, (i + 1) * thin)
        seen[odd_at + i] = got_ref[10, :, span] * live
        seen[even_at + i] = even_ref[10, :, span]
    for i, ref in ((2, coarse_k), (3, coarse_g)):
        span = slice(i * thin, (i + 1) * thin)
        ref[near] = got_ref[10, :, span]
        ref[far] = even_ref[10, :, span]
    coarse_sweep(seen, half, coarse_k, coarse_g, 1, small + 3, 2, small, low_side, live, edges)
    first = lax.axis_index("tm") == 0
    for r in range(small):
        tiles = coarse_row(half, 2 + r, coarse_k, coarse_g, 2 + r, thin, edges)
        for i, tile in enumerate(tiles):
            span = slice(i * LANES, (i + 1) * LANES)
            jump_ref[r, :, span] = end_ref[r, :, span] - jnp.where(first, 0.0, tile)


def fill_coarse(wide, own, even_part, odd_part, reach, low_side, live):
    rows = own.shape[0]
    count = even_part.shape[0]
    for r in range(rows):
        wide[reach + r] = own[r]
    odd_at = jnp.where(low_side, 0, reach + rows)
    even_at = jnp.where(low_side, reach + rows, 0)
    odd_from = jnp.where(low_side, count - reach, 0)
    even_from = jnp.where(low_side, 0, count - reach)
    for i in range(reach):
        wide[odd_at + i] = odd_part[odd_from + i] * live
        wide[even_at + i] = even_part[even_from + i]


def coarse_sweep(source, target, coef_k, coef_g, low, high, reach, rows, low_side, live, edges, shift=0):
    breadth = source.shape[2]
    for row in range(low, high):
        tiles = coarse_row(source, row, coef_k, coef_g, row + shift, breadth, edges)
        if row < reach:
            factor = jnp.where(low_side, live, 1.0)
            tiles = [t * factor for t in tiles]
        elif row >= reach + rows:
            factor = jnp.where(low_side, 1.0, live)
            tiles = [t * factor for t in tiles]
        put_tiles(target, row, tiles)


def edge(steps, coefs, got, even_got, end, coarse):
    breadth = got.shape[2]
    small = end.shape[0]
    wide = pltpu.VMEM((12, 8, breadth), F32)
    thin = pltpu.VMEM((small + 4, 8, breadth // 4), F32)
    return pl.pallas_call(
        edge_kernel,
        out_shape=[
            struct(4, 8, breadth),
            struct(small, 8, breadth // 4),
            struct(small, 8, breadth // 4),
        ],
        in_specs=[VMEM] * 6,
        out_specs=[VMEM] * 3,
        scratch_shapes=[wide] * 7 + [thin] * 4,
        compiler_params=params(16),
        name="edge_updates",
    )(steps, coefs, got, even_got, end, coarse)


def last_kernel(
    fine_hbm, rows_ref, end_ref, jump_ref, before_ref, even_j, odd_j, coarse_ref, even_c, odd_c, out_hbm,
    fine_ref, out_ref, one, two, coarse_k, coarse_g, added, change, moved, sems,
):
    behind = before_ref.shape[0]
    reach = COARSE * behind
    height, breadth = out_hbm.shape[2:]
    columns = breadth // LANES
    small = height // 4
    fetch = pltpu.make_async_copy(fine_hbm, fine_ref, sems.at[8])
    fetch.start()
    low_side = parity() == 0
    live = alive()
    edges = masks()
    slice_id = lax.axis_index("tm")
    fill_coarse(coarse_k, coarse_ref.at[1], even_c.at[0], odd_c.at[0], reach, low_side, live)
    fill_coarse(coarse_g, coarse_ref.at[2], even_c.at[1], odd_c.at[1], reach, low_side, live)
    at = 0
    for j in range(behind):
        width = reach - COARSE * j
        ok = jnp.where(slice_id >= behind - j, 1.0, 0.0).astype(F32)
        target = one if j == 0 else added
        base = reach - width
        for r in range(small):
            target[reach + r] = before_ref[j, r] * ok
        odd_at = jnp.where(low_side, base, reach + small)
        even_at = jnp.where(low_side, reach + small, base)
        for i in range(width):
            target[odd_at + i] = odd_j[at + i] * (ok * live)
            target[even_at + i] = even_j[at + i] * ok
        at += width
        if j > 0:
            for r in range(base, reach + small + width):
                one[r] = one[r] + added[r]
        coarse_sweep(one, two, coarse_k, coarse_g, base + 1, reach + small + width - 1, reach, small, low_side, live, edges)
        coarse_sweep(two, one, coarse_k, coarse_g, base + 2, reach + small + width - 2, reach, small, low_side, live, edges)
    for r in range(small):
        change[:, r, :] = (one[reach + r] + jump_ref[r]) - end_ref[r]
    spread = spread_matrix(breadth)
    moved[...] = split_dot(change[...].reshape(8 * small, breadth // 4), spread).reshape(8, small, breadth)
    fetch.wait()

    def fix(row):
        for x in range(columns):
            for i in range(4):
                fine_ref[:, x, row + i, :] = rows_ref[i, :, x * LANES : (x + 1) * LANES]

    @pl.when(low_side)
    def _():
        fix(8)

    @pl.when(jnp.logical_not(low_side))
    def _():
        fix(8 + height - 4)

    lower = lax.broadcasted_iota(jnp.int32, (8, LANES), 0) < 4

    def body(z, carry):
        for x in range(columns):
            span = slice(x * LANES, (x + 1) * LANES)
            for row in range(0, height, 8):
                c = row // 4
                step = jnp.where(lower, moved[z, c : c + 1, span], moved[z, c + 1 : c + 2, span])
                out_ref[z, row : row + 8, span] = fine_ref[z, x, 8 + row : 16 + row, :] + step
        pltpu.make_async_copy(out_ref.at[z], out_hbm.at[0, z], sems.at[z]).start()
        return carry

    lax.fori_loop(0, 8, body, 0)
    for z in range(8):
        pltpu.make_async_copy(out_ref.at[z], out_hbm.at[0, z], sems.at[z]).wait()


def last(fine, rows, end, jump, before, even_j, odd_j, coarse, even_c, odd_c, height):
    breadth = rows.shape[2]
    small = height // 4
    reach = COARSE * before.shape[0]
    thin = pltpu.VMEM((small + 2 * reach, 8, breadth // 4), F32)
    return pl.pallas_call(
        last_kernel,
        out_shape=struct(1, 8, height, breadth),
        in_specs=[ANY] + [VMEM] * 9,
        out_specs=HBM,
        scratch_shapes=[pltpu.VMEM(fine.shape, F32), pltpu.VMEM((8, height, breadth), F32)]
        + [thin] * 5
        + [
            pltpu.VMEM((8, small, breadth // 4), F32),
            pltpu.VMEM((8, small, breadth), F32),
            pltpu.SemaphoreType.DMA((9,)),
        ],
        compiler_params=params(16),
        name="chain_and_spread",
    )(fine, rows, end, jump, before, even_j, odd_j, coarse, even_c, odd_c)


def relay(jump, coarse, even_c, odd_c, even, odd):
    low_side = parity() == 0
    live = alive()
    small = jump.shape[0]

    def widened(own, even_part, odd_part):
        odd_part = odd_part * live
        low = jnp.where(low_side, odd_part, even_part)
        high = jnp.where(low_side, even_part, odd_part)
        return jnp.concatenate([low, own, high], axis=1)

    def update(values, k, g):
        rows = values.shape[0] - 2
        middle = values[1:-1]
        plus = values[2:] + jnp.pad(middle, ((0, 0), (0, 0), (0, 1)))[:, :, 1:]
        minus = values[:-2] + jnp.pad(middle, ((0, 0), (0, 0), (1, 0)))[:, :, :-1]
        levels = jnp.pad(middle, ((0, 0), (0, 1), (0, 0)))[:, 1:] + jnp.pad(middle, ((0, 0), (1, 0), (0, 0)))[:, :-1]
        bend = levels - 2.0 * middle + (plus + minus - 4.0 * middle) / 16.0
        drift = VEL * (plus - minus) / 8.0
        return middle + (k * bend - 2.0 * DT * drift + g * (middle - middle * middle * middle / 3.0))

    coefs = widened(coarse[1:], even_c, odd_c)
    place = lax.axis_index("space")
    start = jnp.where(place == 0, 1, 0)
    stop = jnp.where(place == lax.axis_size("space") - 1, small + 1, small + 2)
    row = jnp.arange(small + 2)[:, None, None]
    inside = jnp.logical_and(row >= start, row < stop)

    def advance(values):
        block = values[None]
        even_v = lax.ppermute(rows_for(block, jnp.logical_not(low_side), 2), "space", even)
        odd_v = lax.ppermute(rows_for(block, low_side, 2), "space", odd)
        wide = widened(block, even_v, odd_v)[0]
        wide = jnp.where(inside, update(wide, coefs[0, 1:-1], coefs[1, 1:-1]), 0.0)
        return update(wide, coarse[1], coarse[2])

    slice_id = lax.axis_index("tm")
    slices = lax.axis_size("tm")
    onward = [(i, i + 1) for i in range(slices - 1)]

    def link(position, state):
        incoming = lax.ppermute(state, "tm", onward)
        return jnp.where(slice_id > 0, advance(incoming), 0.0) + jump

    return lax.fori_loop(0, slices - 1, link, jump)


def per_device(starts, diffusivity, reaction):
    height, breadth = starts.shape[2:]
    small = height // 4
    slices = lax.axis_size("tm")
    behind = slices - 1
    reach = COARSE * behind
    at_once = 0 < behind and reach <= small
    even, odd = exchanges(lax.axis_size("space"))
    low_side = parity() == 0
    high_side = jnp.logical_not(low_side)

    even_rows, odd_rows = pack(starts, diffusivity, reaction)
    odd_got = lax.ppermute(odd_rows, "space", odd)
    even_got = lax.ppermute(even_rows, "space", even)
    fine, steps, coefs, coarse, end = inner(starts, diffusivity, reaction, even_got)
    rows, end, jump = edge(steps, coefs, odd_got, even_got, end, coarse)
    width = reach if at_once else COARSE
    later, jump = lax.optimization_barrier((coarse[1:], jump))
    odd_c = lax.ppermute(rows_for(later, low_side, width), "space", odd)
    even_c = lax.ppermute(rows_for(later, high_side, width), "space", even)
    if at_once:
        before = [
            lax.ppermute(jump, "tm", [(i, (i + k) % slices) for i in range(slices)])
            for k in range(behind, 0, -1)
        ]
        before = jnp.stack(before)

        def outer(low):
            return jnp.concatenate(
                [rows_for(before[j][None], low, reach - COARSE * j)[0] for j in range(behind)], axis=0
            )

        odd_j = lax.ppermute(outer(low_side), "space", odd)
        even_j = lax.ppermute(outer(high_side), "space", even)
        return last(fine, rows, end, jump, before, even_j, odd_j, coarse, even_c, odd_c, height)
    chained = relay(jump, coarse, even_c, odd_c, even, odd)
    change = jnp.repeat(jnp.repeat(jnp.transpose(chained - end, (1, 0, 2)), 4, axis=1), 4, axis=2)
    fixed = jnp.where(low_side, 0, height - 4)
    fine = jnp.transpose(fine[:, :, 8 : 8 + height], (0, 2, 1, 3)).reshape(8, height, breadth)
    fine = lax.dynamic_update_slice_in_dim(fine, jnp.transpose(rows, (1, 0, 2)), fixed, axis=1)
    return (fine + change)[None]


def solution(mesh):
    in_specs = (P("tm", None, "space", None), P(None, "space", None), P(None, "space", None))
    out_specs = P("tm", None, "space", None)
    return jax.shard_map(per_device, mesh=mesh, in_specs=in_specs, out_specs=out_specs, check_vma=False)
```

```python
import functools

import jax
import jax.numpy as jnp
from jax import lax
from jax.experimental import pallas as pl
from jax.experimental.pallas import tpu as pltpu
from jax.sharding import PartitionSpec as P

FINE = 4
COARSE = 2
DT = 0.05
VEL = 0.5
LANES = 128
F32 = jnp.float32
BF16 = jnp.bfloat16

VMEM = pl.BlockSpec(memory_space=pltpu.VMEM)
ANY = pl.BlockSpec(memory_space=pl.ANY)
HBM = pl.BlockSpec(memory_space=pltpu.HBM)


def params(mib):
    return pltpu.CompilerParams(vmem_limit_bytes=mib * 2**20)


def struct(*shape):
    return jax.ShapeDtypeStruct(shape, F32)


def parity():
    return lax.rem(lax.axis_index("space"), 2)


def tiles_of(ref, row, breadth):
    return [ref[row, :, i : i + LANES] for i in range(0, breadth, LANES)]


def put_tiles(ref, row, tiles):
    for i, tile in enumerate(tiles):
        ref[row, :, i * LANES : (i + 1) * LANES] = tile


def masks():
    lane = lax.broadcasted_iota(jnp.int32, (8, LANES), 1)
    level = lax.broadcasted_iota(jnp.int32, (8, LANES), 0)
    return lane == 0, lane == LANES - 1, level == 0, level == 7


def neighbours(tiles, edges):
    first, last, bottom, top = edges
    back = [pltpu.roll(t, LANES - 1, 1) for t in tiles]
    forth = [pltpu.roll(t, 1, 1) for t in tiles]
    zero = jnp.zeros_like(tiles[0])
    x_next = [jnp.where(last, b, a) for a, b in zip(back, back[1:] + [zero])]
    x_prev = [jnp.where(first, b, a) for a, b in zip(forth, [zero] + forth[:-1])]
    levels = [
        jnp.where(top, 0.0, pltpu.roll(t, 7, 0)) + jnp.where(bottom, 0.0, pltpu.roll(t, 1, 0))
        for t in tiles
    ]
    return x_next, x_prev, levels


def fine_row(state, row, coef_a, coef_b, coef_k, coef_row, breadth, edges):
    tiles = tiles_of(state, row, breadth)
    x_next, x_prev, levels = neighbours(tiles, edges)
    out = []
    for i, u in enumerate(tiles):
        span = slice(i * LANES, (i + 1) * LANES)
        plus = state[row + 1, :, span] + x_next[i]
        minus = state[row - 1, :, span] + x_prev[i]
        own = u * (coef_a[coef_row, :, span] - coef_b[coef_row, :, span] * (u * u))
        spread = coef_k[coef_row, :, span] * ((plus + minus) + levels[i])
        out.append((own + spread) - (0.5 * VEL * DT) * (plus - minus))
    return out


def coarse_row(state, row, coef_k, coef_g, coef_row, breadth, edges):
    tiles = tiles_of(state, row, breadth)
    x_next, x_prev, levels = neighbours(tiles, edges)
    out = []
    for i, c in enumerate(tiles):
        span = slice(i * LANES, (i + 1) * LANES)
        plus = state[row + 1, :, span] + x_next[i]
        minus = state[row - 1, :, span] + x_prev[i]
        k = coef_k[coef_row, :, span]
        g = coef_g[coef_row, :, span]
        bend = (levels[i] - 2.0 * c) + ((plus + minus) - 4.0 * c) * (1.0 / 16.0)
        drift = (2.0 * DT * VEL / 8.0) * (plus - minus)
        out.append(c + ((k * bend - drift) + g * (c - c * c * c * (1.0 / 3.0))))
    return out


def split_dot(values, matrix):
    high = values.astype(BF16)
    low = (values - high.astype(F32)).astype(BF16)
    both = jnp.dot(jnp.concatenate([high, low], axis=0), matrix, preferred_element_type=F32)
    rows = values.shape[0]
    return both[:rows] + both[rows:]


def pool_matrix(breadth, value):
    fine = lax.broadcasted_iota(jnp.int32, (breadth, breadth // 4), 0)
    coarse = lax.broadcasted_iota(jnp.int32, (breadth, breadth // 4), 1)
    return jnp.where(fine // 4 == coarse, value, 0.0).astype(BF16)


def spread_matrix(breadth):
    coarse = lax.broadcasted_iota(jnp.int32, (breadth // 4, breadth), 0)
    fine = lax.broadcasted_iota(jnp.int32, (breadth // 4, breadth), 1)
    return jnp.where(fine // 4 == coarse, 1.0, 0.0).astype(BF16)


def pooled(ref, first_row, coarse_rows, pool):
    sums = []
    for c in range(coarse_rows):
        r = first_row + 4 * c
        sums.append((ref[r] + ref[r + 1]) + (ref[r + 2] + ref[r + 3]))
    return split_dot(jnp.concatenate(sums, axis=0), pool)


def set_coefs(k, g, a_ref, b_ref, k_ref, row):
    k = DT * k
    g = DT * g
    k_ref[row] = k
    b_ref[row] = g * (1.0 / 3.0)
    a_ref[row] = 1.0 + (g - 6.0 * k)


def pack_kernel(
    u_hbm, k_hbm, g_hbm, odd_ref, even_ref, u_nat, k_nat, g_nat, k_wide, g_wide, state, after, coef_a, coef_b, coef_k, sems
):
    height, breadth = u_hbm.shape[2:]
    copies = []
    for side, (low, low16) in enumerate(((0, 0), (height - 8, height - 16))):
        copies.append(pltpu.make_async_copy(u_hbm.at[0, :, pl.ds(low, 8), :], u_nat.at[side], sems.at[0, side]))
        copies.append(pltpu.make_async_copy(k_hbm.at[:, pl.ds(low16, 16), :], k_nat.at[side], sems.at[1, side]))
        copies.append(pltpu.make_async_copy(g_hbm.at[:, pl.ds(low16, 16), :], g_nat.at[side], sems.at[2, side]))
    for copy in copies:
        copy.start()
    pool = pool_matrix(breadth, 1.0 / 16.0)
    edges = masks()
    zeros = jnp.zeros((8, breadth), F32)
    state[0] = zeros
    state[5] = zeros
    after[0] = zeros
    after[3] = zeros
    for copy in copies:
        copy.wait()

    def rows_of(side):
        k_wide[side] = k_nat[side].astype(F32)
        g_wide[side] = g_nat[side].astype(F32)
        low = 12 if side else 0
        u_rows = [u_nat[side, :, i, :] for i in range(8)]
        k_rows = [k_wide[side, :, low + i, :] for i in range(4)]
        g_rows = [g_wide[side, :, low + i, :] for i in range(4)]
        sums = [(r[0] + r[1]) + (r[2] + r[3]) for r in (u_rows[:4], u_rows[4:], k_rows, g_rows)]
        return u_rows, k_rows, g_rows, sums

    def both(first, second):
        u_rows, k_rows, g_rows, odd_sums = rows_of(first)
        near = 4 if first else 1
        step = -1 if first else 1
        for i in range(4):
            state[1 + i] = u_rows[(4 if first else 0) + i]
            set_coefs(k_rows[i], g_rows[i], coef_a, coef_b, coef_k, 1 + i)
        odd_ref[0] = state[near]
        put_tiles(odd_ref, 1, fine_row(state, near, coef_a, coef_b, coef_k, near, breadth, edges))
        one = fine_row(state, near + step, coef_a, coef_b, coef_k, near + step, breadth, edges)
        two = fine_row(state, near + 2 * step, coef_a, coef_b, coef_k, near + 2 * step, breadth, edges)
        put_tiles(odd_ref, 2, one)
        place = 2 if first else 1
        put_tiles(after, place, one)
        put_tiles(after, place + step, two)
        put_tiles(odd_ref, 3, fine_row(after, place, coef_a, coef_b, coef_k, near + step, breadth, edges))
        odd_ref[4] = k_rows[near - 1]
        odd_ref[5] = g_rows[near - 1]
        odd_ref[6] = k_rows[near - 1 + step]
        u_rows, k_rows, g_rows, even_sums = rows_of(second)
        for i in range(4):
            even_ref[i] = u_rows[(4 if second else 0) + i]
        for i in range(3):
            even_ref[4 + i] = k_rows[(1 if second else 0) + i]
            even_ref[7 + i] = g_rows[(1 if second else 0) + i]
        small = split_dot(jnp.concatenate(odd_sums + even_sums, axis=0), pool)
        for j, ref in enumerate((odd_ref, even_ref)):
            for i in range(4):
                scale = 1.0 if i < 2 else 2.0 * DT
                row = small[32 * j + 8 * i : 32 * j + 8 * i + 8]
                ref[ref.shape[0] - 1, :, i * (breadth // 4) : (i + 1) * (breadth // 4)] = row * scale

    even_device = parity() == 0

    @pl.when(even_device)
    def _():
        both(0, 1)

    @pl.when(jnp.logical_not(even_device))
    def _():
        both(1, 0)


def pack(starts, diffusivity, reaction):
    breadth = starts.shape[3]
    coef = pltpu.VMEM((6, 8, breadth), F32)
    return pl.pallas_call(
        pack_kernel,
        out_shape=[struct(8, 8, breadth), struct(11, 8, breadth)],
        in_specs=[HBM] * 3,
        out_specs=[VMEM] * 2,
        scratch_shapes=[
            pltpu.VMEM((2, 8, 8, breadth), F32),
            pltpu.VMEM((2, 8, 16, breadth), BF16),
            pltpu.VMEM((2, 8, 16, breadth), BF16),
            pltpu.VMEM((2, 8, 16, breadth), F32),
            pltpu.VMEM((2, 8, 16, breadth), F32),
            coef,
            pltpu.VMEM((4, 8, breadth), F32),
            coef,
            coef,
            coef,
            pltpu.SemaphoreType.DMA((3, 2)),
        ],
        compiler_params=params(53),
        name="pack_rows",
    )(starts, diffusivity, reaction)


def inner_kernel(
    u_hbm, k_hbm, g_hbm, got_ref, fine_ref, steps_ref, coefs_ref, coarse_ref, end_ref,
    one, two, coef_a, coef_b, coef_k, k_nat, g_nat, flat, sems,
):
    height, breadth = u_hbm.shape[2:]
    columns = breadth // LANES
    small = height // 4
    thin = breadth // 4
    spans = [slice(x * LANES, (x + 1) * LANES) for x in range(columns)]
    above = parity() == 0
    own = pl.multiple_of(jnp.where(above, 0, 8), 8)
    copies = [
        pltpu.make_async_copy(
            u_hbm.at[0, :, :, pl.ds(x * LANES, LANES)], one.at[pl.ds(1, 8), x, pl.ds(8 + own, height), :], sems.at[x]
        )
        for x in range(columns)
    ]
    k_copy = pltpu.make_async_copy(k_hbm, k_nat, sems.at[columns])
    g_copy = pltpu.make_async_copy(g_hbm, g_nat, sems.at[columns + 1])
    for copy in [k_copy, g_copy] + copies:
        copy.start()
    blank = jnp.zeros((8, LANES), F32)
    top = height + 16

    def clear(z, carry):
        for ref in (one, two):
            for x in range(columns):
                ref[z, x, 0:8, :] = blank
                ref[z, x, top : top + 8, :] = blank
        return carry

    lax.fori_loop(0, 10, clear, 0)
    for ref in (one, two):
        for z in (0, 9):
            for x in range(columns):
                ref[z, x, 8:top, :] = jnp.zeros((height + 8, LANES), F32)

    def place(u_row, c_row, tile):
        for x in range(columns):
            for z in range(8):
                one[1 + z, x, 8 + tile : 16 + tile, :] = blank
                coef_a[z, x, tile : tile + 8, :] = blank
                coef_b[z, x, tile : tile + 8, :] = blank
                coef_k[z, x, tile : tile + 8, :] = blank
        for x, span in enumerate(spans):
            for i in range(4):
                one[1:9, x, u_row + i, :] = got_ref[i, :, span]
            for i in range(3):
                k = DT * got_ref[4 + i, :, span]
                g = DT * got_ref[7 + i, :, span]
                coef_k[:, x, c_row + i, :] = k
                coef_b[:, x, c_row + i, :] = g * (1.0 / 3.0)
                coef_a[:, x, c_row + i, :] = 1.0 + (g - 6.0 * k)

    @pl.when(above)
    def _():
        place(8 + height, height, height)

    @pl.when(jnp.logical_not(above))
    def _():
        place(12, 5, 0)

    k_copy.wait()
    g_copy.wait()

    def widen(z, carry):
        for x, span in enumerate(spans):
            for r in range(0, height, 16):
                k = DT * k_nat[z, r : r + 16, span].astype(F32)
                g = DT * g_nat[z, r : r + 16, span].astype(F32)
                rows = pl.ds(own + r, 16)
                coef_k[z, x, rows, :] = k
                coef_b[z, x, rows, :] = g * (1.0 / 3.0)
                coef_a[z, x, rows, :] = 1.0 + (g - 6.0 * k)
        return carry

    lax.fori_loop(0, 8, widen, 0)
    for copy in copies:
        copy.wait()

    lane = lax.broadcasted_iota(jnp.int32, (8, LANES), 1)
    first, final = lane == 0, lane == LANES - 1

    def sweep(source, target, level, shift):
        def body(z, carry):
            for row in range(8, top, 8):
                tiles = [source[z + 1, x, row : row + 8, :] for x in range(columns)]
                back = [pltpu.roll(t, LANES - 1, 1) for t in tiles] + [blank]
                forth = [blank] + [pltpu.roll(t, 1, 1) for t in tiles]
                for x, u in enumerate(tiles):
                    x_next = jnp.where(final, back[x + 1], back[x])
                    x_prev = jnp.where(first, forth[x], forth[x + 1])
                    plus = source[z + 1, x, row + 1 : row + 9, :] + x_next
                    minus = source[z + 1, x, row - 1 : row + 7, :] + x_prev
                    levels = source[z, x, row : row + 8, :] + source[z + 2, x, row : row + 8, :]
                    rows = slice(row - 8, row)
                    own_part = u * (coef_a[z, x, rows, :] - coef_b[z, x, rows, :] * (u * u))
                    spread = coef_k[z, x, rows, :] * ((plus + minus) + levels)
                    out = (own_part + spread) - (0.5 * VEL * DT) * (plus - minus)
                    if shift is None:
                        target[z + level, x, row : row + 8, :] = out
                    else:
                        target[z + level, x, pl.ds(pl.multiple_of(row + shift, 8), 8), :] = out
            return carry

        lax.fori_loop(0, 8, body, 0, unroll=4)

    def keep(step, source):
        def write(row):
            for x, span in enumerate(spans):
                for i in range(2):
                    steps_ref[2 * step + i, :, span] = source[1:9, x, row + i, :]

        @pl.when(above)
        def _():
            write(8 + step)

        @pl.when(jnp.logical_not(above))
        def _():
            write(16 + height - 2 - step)

    def keep_coefs(row):
        for x, span in enumerate(spans):
            for i in range(4):
                coefs_ref[0, i, :, span] = coef_a[:, x, row + i, :]
                coefs_ref[1, i, :, span] = coef_b[:, x, row + i, :]
                coefs_ref[2, i, :, span] = coef_k[:, x, row + i, :]

    @pl.when(above)
    def _():
        keep_coefs(0)

    @pl.when(jnp.logical_not(above))
    def _():
        keep_coefs(8 + height - 4)

    pool = pool_matrix(breadth, 1.0 / 16.0)

    def sums_of(ref, level, start, part):
        def body(z, carry):
            for x, span in enumerate(spans):
                parts = [ref[z + level, x, pl.ds(start + i, small, stride=4), :] for i in range(4)]
                flat[part, z, :, span] = (parts[0] + parts[1]) + (parts[2] + parts[3])
            return carry

        lax.fori_loop(0, 8, body, 0, unroll=2)

    def pooled_into(targets, scales):
        count = len(targets)
        means = split_dot(flat[0:count].reshape(count * 8 * small, breadth), pool).reshape(count, 8, small, thin)
        for part in range(count):
            flat[part, :, :, 0:thin] = means[part] * scales[part]
            for r in range(small):
                targets[part][r] = flat[part, :, r, 0:thin]

    sums_of(one, 1, 8 + own, 0)
    sums_of(coef_k, 0, own, 1)
    sums_of(coef_b, 0, own, 2)
    pooled_into([coarse_ref.at[0], coarse_ref.at[1], coarse_ref.at[2]], (1.0, 2.0, 6.0))
    keep(0, one)
    sweep(one, two, 1, None)
    keep(1, two)
    sweep(two, one, 1, None)
    keep(2, one)
    sweep(one, two, 1, None)
    keep(3, two)
    sweep(two, fine_ref, 0, jnp.where(above, 0, -8))
    sums_of(fine_ref, 0, 8, 0)
    pooled_into([end_ref], (1.0,))


def inner(starts, diffusivity, reaction, got):
    height, breadth = starts.shape[2:]
    small = height // 4
    columns = breadth // LANES
    wide = pltpu.VMEM((10, columns, height + 24, LANES), F32)
    coef = pltpu.VMEM((8, columns, height + 8, LANES), F32)
    return pl.pallas_call(
        inner_kernel,
        out_shape=[
            struct(8, columns, height + 16, LANES),
            struct(8, 8, breadth),
            struct(3, 4, 8, breadth),
            struct(3, small, 8, breadth // 4),
            struct(small, 8, breadth // 4),
        ],
        in_specs=[ANY] * 3 + [VMEM],
        out_specs=[VMEM] * 5,
        scratch_shapes=[wide, wide, coef, coef, coef]
        + [
            pltpu.VMEM((8, height, breadth), BF16),
            pltpu.VMEM((8, height, breadth), BF16),
            pltpu.VMEM((3, 8, small, breadth), F32),
            pltpu.SemaphoreType.DMA((columns + 2,)),
        ],
        compiler_params=params(28),
        cost_estimate=pl.CostEstimate(flops=30_000_000, bytes_accessed=4_000_000, transcendentals=0),
        name="inner_updates",
    )(starts, diffusivity, reaction, got)


def rows_for(array, low_side, reach):
    start = jnp.where(low_side, 0, array.shape[1] - reach)
    return lax.dynamic_slice_in_dim(array, start, reach, axis=1)


def exchanges(count):
    even = [(i, i ^ 1) for i in range(count)]
    odd = [(i, (i - 1 if i % 2 == 0 else i + 1) % count) for i in range(count)]
    return even, odd


def alive():
    place = lax.axis_index("space")
    last = lax.axis_size("space") - 1
    return jnp.where(jnp.logical_or(place == 0, place == last), 0.0, 1.0).astype(F32)


def edge_kernel(
    steps_ref, coefs_ref, got_ref, even_ref, end_in, coarse_ref, rows_ref, end_ref, jump_ref,
    zero, one, two, three, coef_a, coef_b, coef_k, seen, half, coarse_k, coarse_g,
):
    breadth = got_ref.shape[2]
    small = end_ref.shape[0]
    low_side = parity() == 0
    live = alive()
    edges = masks()
    states = (zero, one, two, three, rows_ref)

    def index(distance):
        return jnp.where(low_side, 4 + distance, 7 - distance)

    for i in range(4):
        coef_a[4 + i] = coefs_ref[0, i]
        coef_b[4 + i] = coefs_ref[1, i]
        coef_k[4 + i] = coefs_ref[2, i]
    set_coefs(got_ref[4], got_ref[5], coef_a, coef_b, coef_k, index(-1))
    zero[index(-1)] = got_ref[0] * live
    one[index(-2)] = got_ref[2] * live
    for step in range(4):
        at = jnp.where(low_side, 4 + step, 6 - step)
        for i in range(2):
            states[step][at + i] = steps_ref[2 * step + i]
    toward = jnp.where(low_side, -0.5 * VEL * DT, 0.5 * VEL * DT)
    one[index(-1)] = (got_ref[1] + (DT * got_ref[4] + toward) * zero[index(0)]) * live
    two[index(-2)] = (got_ref[3] + (DT * got_ref[6] + toward) * one[index(-1)]) * live
    for step in range(1, 5):
        for distance in range(0 if step in (1, 4) else -1, step):
            at = index(distance)
            tiles = fine_row(states[step - 1], at, coef_a, coef_b, coef_k, at, breadth, edges)
            if distance < 0:
                tiles = [t * live for t in tiles]
            put_tiles(states[step], at - 4 if step == 4 else at, tiles)
    pool = pool_matrix(breadth, 1.0 / 16.0)
    end_ref[...] = end_in[...]
    end_ref[jnp.where(low_side, 0, small - 1)] = pooled(rows_ref, 0, 1, pool)

    thin = breadth // 4
    odd_at = jnp.where(low_side, 0, 2 + small)
    even_at = jnp.where(low_side, 2 + small, 0)
    near = jnp.where(low_side, 1, 2 + small)
    far = jnp.where(low_side, 2 + small, 1)
    for r in range(small):
        seen[2 + r] = coarse_ref[0, r]
        coarse_k[2 + r] = coarse_ref[1, r]
        coarse_g[2 + r] = coarse_ref[2, r]
    for i in range(2):
        span = slice(i * thin, (i + 1) * thin)
        seen[odd_at + i] = got_ref[7, :, span] * live
        seen[even_at + i] = even_ref[10, :, span]
    for i, ref in ((2, coarse_k), (3, coarse_g)):
        span = slice(i * thin, (i + 1) * thin)
        ref[near] = got_ref[7, :, span]
        ref[far] = even_ref[10, :, span]
    coarse_sweep(seen, half, coarse_k, coarse_g, 1, small + 3, 2, small, low_side, live, edges)
    first = lax.axis_index("tm") == 0
    for r in range(small):
        tiles = coarse_row(half, 2 + r, coarse_k, coarse_g, 2 + r, thin, edges)
        for i, tile in enumerate(tiles):
            span = slice(i * LANES, (i + 1) * LANES)
            jump_ref[r, :, span] = end_ref[r, :, span] - jnp.where(first, 0.0, tile)


def fill_coarse(wide, own, even_part, odd_part, reach, low_side, live):
    rows = own.shape[0]
    count = even_part.shape[0]
    for r in range(rows):
        wide[reach + r] = own[r]
    odd_at = jnp.where(low_side, 0, reach + rows)
    even_at = jnp.where(low_side, reach + rows, 0)
    odd_from = jnp.where(low_side, count - reach, 0)
    even_from = jnp.where(low_side, 0, count - reach)
    for i in range(reach):
        wide[odd_at + i] = odd_part[odd_from + i] * live
        wide[even_at + i] = even_part[even_from + i]


def coarse_sweep(source, target, coef_k, coef_g, low, high, reach, rows, low_side, live, edges, shift=0):
    breadth = source.shape[2]
    for row in range(low, high):
        tiles = coarse_row(source, row, coef_k, coef_g, row + shift, breadth, edges)
        if row < reach:
            factor = jnp.where(low_side, live, 1.0)
            tiles = [t * factor for t in tiles]
        elif row >= reach + rows:
            factor = jnp.where(low_side, 1.0, live)
            tiles = [t * factor for t in tiles]
        put_tiles(target, row, tiles)


def edge(steps, coefs, got, even_got, end, coarse):
    breadth = got.shape[2]
    small = end.shape[0]
    wide = pltpu.VMEM((12, 8, breadth), F32)
    thin = pltpu.VMEM((small + 4, 8, breadth // 4), F32)
    return pl.pallas_call(
        edge_kernel,
        out_shape=[
            struct(4, 8, breadth),
            struct(small, 8, breadth // 4),
            struct(small, 8, breadth // 4),
        ],
        in_specs=[VMEM] * 6,
        out_specs=[VMEM] * 3,
        scratch_shapes=[wide] * 7 + [thin] * 4,
        compiler_params=params(16),
        name="edge_updates",
    )(steps, coefs, got, even_got, end, coarse)


def last_kernel(
    fine_hbm, rows_ref, end_ref, jump_ref, before_ref, even_j, odd_j, coarse_ref, even_c, odd_c, out_hbm,
    fine_ref, out_ref, one, two, coarse_k, coarse_g, added, change, moved, sems,
):
    behind = before_ref.shape[0]
    reach = COARSE * behind
    height, breadth = out_hbm.shape[2:]
    columns = breadth // LANES
    small = height // 4
    fetch = pltpu.make_async_copy(fine_hbm, fine_ref, sems.at[8])
    fetch.start()
    low_side = parity() == 0
    live = alive()
    edges = masks()
    slice_id = lax.axis_index("tm")
    fill_coarse(coarse_k, coarse_ref.at[1], even_c.at[0], odd_c.at[0], reach, low_side, live)
    fill_coarse(coarse_g, coarse_ref.at[2], even_c.at[1], odd_c.at[1], reach, low_side, live)
    at = 0
    for j in range(behind):
        width = reach - COARSE * j
        ok = jnp.where(slice_id >= behind - j, 1.0, 0.0).astype(F32)
        target = one if j == 0 else added
        base = reach - width
        for r in range(small):
            target[reach + r] = before_ref[j, r] * ok
        odd_at = jnp.where(low_side, base, reach + small)
        even_at = jnp.where(low_side, reach + small, base)
        for i in range(width):
            target[odd_at + i] = odd_j[at + i] * (ok * live)
            target[even_at + i] = even_j[at + i] * ok
        at += width
        if j > 0:
            for r in range(base, reach + small + width):
                one[r] = one[r] + added[r]
        coarse_sweep(one, two, coarse_k, coarse_g, base + 1, reach + small + width - 1, reach, small, low_side, live, edges)
        coarse_sweep(two, one, coarse_k, coarse_g, base + 2, reach + small + width - 2, reach, small, low_side, live, edges)
    for r in range(small):
        change[:, r, :] = (one[reach + r] + jump_ref[r]) - end_ref[r]
    spread = spread_matrix(breadth)
    moved[...] = split_dot(change[...].reshape(8 * small, breadth // 4), spread).reshape(8, small, breadth)
    fetch.wait()

    def fix(row):
        for x in range(columns):
            for i in range(4):
                fine_ref[:, x, row + i, :] = rows_ref[i, :, x * LANES : (x + 1) * LANES]

    @pl.when(low_side)
    def _():
        fix(8)

    @pl.when(jnp.logical_not(low_side))
    def _():
        fix(8 + height - 4)

    lower = lax.broadcasted_iota(jnp.int32, (8, LANES), 0) < 4

    def body(z, carry):
        for x in range(columns):
            span = slice(x * LANES, (x + 1) * LANES)
            for row in range(0, height, 8):
                c = row // 4
                step = jnp.where(lower, moved[z, c : c + 1, span], moved[z, c + 1 : c + 2, span])
                out_ref[z, row : row + 8, span] = fine_ref[z, x, 8 + row : 16 + row, :] + step
        pltpu.make_async_copy(out_ref.at[z], out_hbm.at[0, z], sems.at[z]).start()
        return carry

    lax.fori_loop(0, 8, body, 0)
    for z in range(8):
        pltpu.make_async_copy(out_ref.at[z], out_hbm.at[0, z], sems.at[z]).wait()


def last(fine, rows, end, jump, before, even_j, odd_j, coarse, even_c, odd_c, height):
    breadth = rows.shape[2]
    small = height // 4
    reach = COARSE * before.shape[0]
    thin = pltpu.VMEM((small + 2 * reach, 8, breadth // 4), F32)
    return pl.pallas_call(
        last_kernel,
        out_shape=struct(1, 8, height, breadth),
        in_specs=[ANY] + [VMEM] * 9,
        out_specs=HBM,
        scratch_shapes=[pltpu.VMEM(fine.shape, F32), pltpu.VMEM((8, height, breadth), F32)]
        + [thin] * 5
        + [
            pltpu.VMEM((8, small, breadth // 4), F32),
            pltpu.VMEM((8, small, breadth), F32),
            pltpu.SemaphoreType.DMA((9,)),
        ],
        compiler_params=params(16),
        name="chain_and_spread",
    )(fine, rows, end, jump, before, even_j, odd_j, coarse, even_c, odd_c)


def relay(jump, coarse, even_c, odd_c, even, odd):
    low_side = parity() == 0
    live = alive()
    small = jump.shape[0]

    def widened(own, even_part, odd_part):
        odd_part = odd_part * live
        low = jnp.where(low_side, odd_part, even_part)
        high = jnp.where(low_side, even_part, odd_part)
        return jnp.concatenate([low, own, high], axis=1)

    def update(values, k, g):
        rows = values.shape[0] - 2
        middle = values[1:-1]
        plus = values[2:] + jnp.pad(middle, ((0, 0), (0, 0), (0, 1)))[:, :, 1:]
        minus = values[:-2] + jnp.pad(middle, ((0, 0), (0, 0), (1, 0)))[:, :, :-1]
        levels = jnp.pad(middle, ((0, 0), (0, 1), (0, 0)))[:, 1:] + jnp.pad(middle, ((0, 0), (1, 0), (0, 0)))[:, :-1]
        bend = levels - 2.0 * middle + (plus + minus - 4.0 * middle) / 16.0
        drift = VEL * (plus - minus) / 8.0
        return middle + (k * bend - 2.0 * DT * drift + g * (middle - middle * middle * middle / 3.0))

    coefs = widened(coarse[1:], even_c, odd_c)
    place = lax.axis_index("space")
    start = jnp.where(place == 0, 1, 0)
    stop = jnp.where(place == lax.axis_size("space") - 1, small + 1, small + 2)
    row = jnp.arange(small + 2)[:, None, None]
    inside = jnp.logical_and(row >= start, row < stop)

    def advance(values):
        block = values[None]
        even_v = lax.ppermute(rows_for(block, jnp.logical_not(low_side), 2), "space", even)
        odd_v = lax.ppermute(rows_for(block, low_side, 2), "space", odd)
        wide = widened(block, even_v, odd_v)[0]
        wide = jnp.where(inside, update(wide, coefs[0, 1:-1], coefs[1, 1:-1]), 0.0)
        return update(wide, coarse[1], coarse[2])

    slice_id = lax.axis_index("tm")
    slices = lax.axis_size("tm")
    onward = [(i, i + 1) for i in range(slices - 1)]

    def link(position, state):
        incoming = lax.ppermute(state, "tm", onward)
        return jnp.where(slice_id > 0, advance(incoming), 0.0) + jump

    return lax.fori_loop(0, slices - 1, link, jump)


def per_device(starts, diffusivity, reaction):
    height, breadth = starts.shape[2:]
    small = height // 4
    slices = lax.axis_size("tm")
    behind = slices - 1
    reach = COARSE * behind
    at_once = 0 < behind and reach <= small
    even, odd = exchanges(lax.axis_size("space"))
    low_side = parity() == 0
    high_side = jnp.logical_not(low_side)

    odd_rows, even_rows = pack(starts, diffusivity, reaction)
    odd_got = lax.ppermute(odd_rows, "space", odd)
    even_got = lax.ppermute(even_rows, "space", even)
    fine, steps, coefs, coarse, end = inner(starts, diffusivity, reaction, even_got)
    rows, end, jump = edge(steps, coefs, odd_got, even_got, end, coarse)
    width = reach if at_once else COARSE
    later, jump = lax.optimization_barrier((coarse[1:], jump))
    odd_c = lax.ppermute(rows_for(later, low_side, width), "space", odd)
    even_c = lax.ppermute(rows_for(later, high_side, width), "space", even)
    if at_once:
        before = [
            lax.ppermute(jump, "tm", [(i, (i + k) % slices) for i in range(slices)])
            for k in range(behind, 0, -1)
        ]
        before = jnp.stack(before)

        def outer(low):
            return jnp.concatenate(
                [rows_for(before[j][None], low, reach - COARSE * j)[0] for j in range(behind)], axis=0
            )

        odd_j = lax.ppermute(outer(low_side), "space", odd)
        even_j = lax.ppermute(outer(high_side), "space", even)
        return last(fine, rows, end, jump, before, even_j, odd_j, coarse, even_c, odd_c, height)
    chained = relay(jump, coarse, even_c, odd_c, even, odd)
    change = jnp.repeat(jnp.repeat(jnp.transpose(chained - end, (1, 0, 2)), 4, axis=1), 4, axis=2)
    fixed = jnp.where(low_side, 0, height - 4)
    fine = jnp.transpose(fine[:, :, 8 : 8 + height], (0, 2, 1, 3)).reshape(8, height, breadth)
    fine = lax.dynamic_update_slice_in_dim(fine, jnp.transpose(rows, (1, 0, 2)), fixed, axis=1)
    return (fine + change)[None]


def solution(mesh):
    in_specs = (P("tm", None, "space", None), P(None, "space", None), P(None, "space", None))
    out_specs = P("tm", None, "space", None)
    return jax.shard_map(per_device, mesh=mesh, in_specs=in_specs, out_specs=out_specs, check_vma=False)
```

```python
import functools

import jax
import jax.numpy as jnp
from jax import lax
from jax.experimental import pallas as pl
from jax.experimental.pallas import tpu as pltpu
from jax.sharding import PartitionSpec as P

FINE = 4
COARSE = 2
DT = 0.05
VEL = 0.5
LANES = 128
F32 = jnp.float32
BF16 = jnp.bfloat16
ODD_MIB = 53.4

VMEM = pl.BlockSpec(memory_space=pltpu.VMEM)
ANY = pl.BlockSpec(memory_space=pl.ANY)
HBM = pl.BlockSpec(memory_space=pltpu.HBM)


def params(mib):
    return pltpu.CompilerParams(vmem_limit_bytes=int(mib * 2**20))


def struct(*shape):
    return jax.ShapeDtypeStruct(shape, F32)


def parity():
    return lax.rem(lax.axis_index("space"), 2)


def tiles_of(ref, row, breadth):
    return [ref[row, :, i : i + LANES] for i in range(0, breadth, LANES)]


def put_tiles(ref, row, tiles):
    for i, tile in enumerate(tiles):
        ref[row, :, i * LANES : (i + 1) * LANES] = tile


def masks():
    lane = lax.broadcasted_iota(jnp.int32, (8, LANES), 1)
    level = lax.broadcasted_iota(jnp.int32, (8, LANES), 0)
    return lane == 0, lane == LANES - 1, level == 0, level == 7


def neighbours(tiles, edges):
    first, last, bottom, top = edges
    back = [pltpu.roll(t, LANES - 1, 1) for t in tiles]
    forth = [pltpu.roll(t, 1, 1) for t in tiles]
    zero = jnp.zeros_like(tiles[0])
    x_next = [jnp.where(last, b, a) for a, b in zip(back, back[1:] + [zero])]
    x_prev = [jnp.where(first, b, a) for a, b in zip(forth, [zero] + forth[:-1])]
    levels = [
        jnp.where(top, 0.0, pltpu.roll(t, 7, 0)) + jnp.where(bottom, 0.0, pltpu.roll(t, 1, 0))
        for t in tiles
    ]
    return x_next, x_prev, levels


def fine_row(state, row, coef_a, coef_b, coef_k, coef_row, breadth, edges):
    tiles = tiles_of(state, row, breadth)
    x_next, x_prev, levels = neighbours(tiles, edges)
    out = []
    for i, u in enumerate(tiles):
        span = slice(i * LANES, (i + 1) * LANES)
        plus = state[row + 1, :, span] + x_next[i]
        minus = state[row - 1, :, span] + x_prev[i]
        own = u * (coef_a[coef_row, :, span] - coef_b[coef_row, :, span] * (u * u))
        spread = coef_k[coef_row, :, span] * ((plus + minus) + levels[i])
        out.append((own + spread) - (0.5 * VEL * DT) * (plus - minus))
    return out


def coarse_row(state, row, coef_k, coef_g, coef_row, breadth, edges):
    tiles = tiles_of(state, row, breadth)
    x_next, x_prev, levels = neighbours(tiles, edges)
    out = []
    for i, c in enumerate(tiles):
        span = slice(i * LANES, (i + 1) * LANES)
        plus = state[row + 1, :, span] + x_next[i]
        minus = state[row - 1, :, span] + x_prev[i]
        k = coef_k[coef_row, :, span]
        g = coef_g[coef_row, :, span]
        bend = (levels[i] - 2.0 * c) + ((plus + minus) - 4.0 * c) * (1.0 / 16.0)
        drift = (2.0 * DT * VEL / 8.0) * (plus - minus)
        out.append(c + ((k * bend - drift) + g * (c - c * c * c * (1.0 / 3.0))))
    return out


def split_dot(values, matrix):
    high = values.astype(BF16)
    low = (values - high.astype(F32)).astype(BF16)
    both = jnp.dot(jnp.concatenate([high, low], axis=0), matrix, preferred_element_type=F32)
    rows = values.shape[0]
    return both[:rows] + both[rows:]


def pool_matrix(breadth, value):
    fine = lax.broadcasted_iota(jnp.int32, (breadth, breadth // 4), 0)
    coarse = lax.broadcasted_iota(jnp.int32, (breadth, breadth // 4), 1)
    return jnp.where(fine // 4 == coarse, value, 0.0).astype(BF16)


def spread_matrix(breadth):
    coarse = lax.broadcasted_iota(jnp.int32, (breadth // 4, breadth), 0)
    fine = lax.broadcasted_iota(jnp.int32, (breadth // 4, breadth), 1)
    return jnp.where(fine // 4 == coarse, 1.0, 0.0).astype(BF16)


def pooled(ref, first_row, coarse_rows, pool):
    sums = []
    for c in range(coarse_rows):
        r = first_row + 4 * c
        sums.append((ref[r] + ref[r + 1]) + (ref[r + 2] + ref[r + 3]))
    return split_dot(jnp.concatenate(sums, axis=0), pool)


def set_coefs(k, g, a_ref, b_ref, k_ref, row):
    k = DT * k
    g = DT * g
    k_ref[row] = k
    b_ref[row] = g * (1.0 / 3.0)
    a_ref[row] = 1.0 + (g - 6.0 * k)


def put_pooled(ref, sums, pool):
    thin = ref.shape[2] // 4
    small = split_dot(jnp.concatenate(sums, axis=0), pool)
    for i in range(4):
        row = small[8 * i : 8 * i + 8] * (1.0 if i < 2 else 2.0 * DT)
        ref[ref.shape[0] - 1, :, i * thin : (i + 1) * thin] = row


def sums_of_four(*arrays):
    return [(r[0] + r[1]) + (r[2] + r[3]) for r in arrays]


def odd_kernel(
    u_hbm, k_hbm, g_hbm, odd_ref, u_nat, k_nat, g_nat, k_wide, g_wide, state, after, coef_a, coef_b, coef_k, sems
):
    height, breadth = u_hbm.shape[2:]
    low_side = parity() == 0
    row8 = pl.multiple_of(jnp.where(low_side, 0, height - 8), 8)
    row16 = pl.multiple_of(jnp.where(low_side, 0, height - 16), 16)
    copies = [
        pltpu.make_async_copy(u_hbm.at[0, :, pl.ds(row8, 8), :], u_nat, sems.at[0]),
        pltpu.make_async_copy(k_hbm.at[:, pl.ds(row16, 16), :], k_nat, sems.at[1]),
        pltpu.make_async_copy(g_hbm.at[:, pl.ds(row16, 16), :], g_nat, sems.at[2]),
    ]
    for copy in copies:
        copy.start()
    pool = pool_matrix(breadth, 1.0 / 16.0)
    edges = masks()
    zeros = jnp.zeros((8, breadth), F32)
    state[0] = zeros
    state[5] = zeros
    after[0] = zeros
    after[3] = zeros
    for copy in copies:
        copy.wait()
    k_wide[...] = k_nat[...].astype(F32)
    g_wide[...] = g_nat[...].astype(F32)

    def fill(high):
        low = 12 if high else 0
        u_rows = [u_nat[:, i, :] for i in range(8)]
        k_rows = [k_wide[:, low + i, :] for i in range(4)]
        g_rows = [g_wide[:, low + i, :] for i in range(4)]
        near = 4 if high else 1
        step = -1 if high else 1
        for i in range(4):
            state[1 + i] = u_rows[(4 if high else 0) + i]
            set_coefs(k_rows[i], g_rows[i], coef_a, coef_b, coef_k, 1 + i)
        odd_ref[0] = state[near]
        put_tiles(odd_ref, 1, fine_row(state, near, coef_a, coef_b, coef_k, near, breadth, edges))
        one = fine_row(state, near + step, coef_a, coef_b, coef_k, near + step, breadth, edges)
        two = fine_row(state, near + 2 * step, coef_a, coef_b, coef_k, near + 2 * step, breadth, edges)
        put_tiles(odd_ref, 2, one)
        place = 2 if high else 1
        put_tiles(after, place, one)
        put_tiles(after, place + step, two)
        put_tiles(odd_ref, 3, fine_row(after, place, coef_a, coef_b, coef_k, near + step, breadth, edges))
        odd_ref[4] = k_rows[near - 1]
        odd_ref[5] = g_rows[near - 1]
        odd_ref[6] = k_rows[near - 1 + step]
        put_pooled(odd_ref, sums_of_four(u_rows[:4], u_rows[4:], k_rows, g_rows), pool)

    @pl.when(low_side)
    def _():
        fill(0)

    @pl.when(jnp.logical_not(low_side))
    def _():
        fill(1)


def odd_pack(starts, diffusivity, reaction):
    breadth = starts.shape[3]
    coef = pltpu.VMEM((6, 8, breadth), F32)
    return pl.pallas_call(
        odd_kernel,
        out_shape=struct(8, 8, breadth),
        in_specs=[HBM] * 3,
        out_specs=VMEM,
        scratch_shapes=[
            pltpu.VMEM((8, 8, breadth), F32),
            pltpu.VMEM((8, 16, breadth), BF16),
            pltpu.VMEM((8, 16, breadth), BF16),
            pltpu.VMEM((8, 16, breadth), F32),
            pltpu.VMEM((8, 16, breadth), F32),
            coef,
            pltpu.VMEM((4, 8, breadth), F32),
            coef,
            coef,
            coef,
            pltpu.SemaphoreType.DMA((3,)),
        ],
        compiler_params=params(ODD_MIB),
        name="odd_rows",
    )(starts, diffusivity, reaction)


def even_kernel(odd_rows, u_ref, k_ref, g_ref, even_ref, k_wide, g_wide):
    del odd_rows
    height, breadth = u_ref.shape[2:]
    pool = pool_matrix(breadth, 1.0 / 16.0)

    def fill(high):
        k_wide[...] = k_ref[:, height - 16 if high else 0 : height if high else 16, :].astype(F32)
        g_wide[...] = g_ref[:, height - 16 if high else 0 : height if high else 16, :].astype(F32)
        low = 12 if high else 0
        u_rows = [u_ref[0, :, (height - 8 if high else 0) + i, :] for i in range(8)]
        k_rows = [k_wide[:, low + i, :] for i in range(4)]
        g_rows = [g_wide[:, low + i, :] for i in range(4)]
        for i in range(4):
            even_ref[i] = u_rows[(4 if high else 0) + i]
        for i in range(3):
            even_ref[4 + i] = k_rows[(1 if high else 0) + i]
            even_ref[7 + i] = g_rows[(1 if high else 0) + i]
        put_pooled(even_ref, sums_of_four(u_rows[:4], u_rows[4:], k_rows, g_rows), pool)

    above = parity() == 0

    @pl.when(above)
    def _():
        fill(1)

    @pl.when(jnp.logical_not(above))
    def _():
        fill(0)


def even_pack(odd_rows, starts, diffusivity, reaction):
    breadth = starts.shape[3]
    return pl.pallas_call(
        even_kernel,
        out_shape=struct(11, 8, breadth),
        in_specs=[ANY] + [VMEM] * 3,
        out_specs=VMEM,
        scratch_shapes=[pltpu.VMEM((8, 16, breadth), F32)] * 2,
        compiler_params=params(16),
        name="even_rows",
    )(odd_rows, starts, diffusivity, reaction)


def inner_kernel(
    u_hbm, k_hbm, g_hbm, got_ref, fine_ref, steps_ref, coefs_ref, coarse_ref, end_ref,
    one, two, coef_a, coef_b, coef_k, k_nat, g_nat, flat, sems,
):
    height, breadth = u_hbm.shape[2:]
    columns = breadth // LANES
    small = height // 4
    thin = breadth // 4
    spans = [slice(x * LANES, (x + 1) * LANES) for x in range(columns)]
    above = parity() == 0
    own = pl.multiple_of(jnp.where(above, 0, 8), 8)
    copies = [
        pltpu.make_async_copy(
            u_hbm.at[0, :, :, pl.ds(x * LANES, LANES)], one.at[pl.ds(1, 8), x, pl.ds(8 + own, height), :], sems.at[x]
        )
        for x in range(columns)
    ]
    k_copy = pltpu.make_async_copy(k_hbm, k_nat, sems.at[columns])
    g_copy = pltpu.make_async_copy(g_hbm, g_nat, sems.at[columns + 1])
    for copy in [k_copy, g_copy] + copies:
        copy.start()
    blank = jnp.zeros((8, LANES), F32)
    top = height + 16

    def clear(z, carry):
        for ref in (one, two):
            for x in range(columns):
                ref[z, x, 0:8, :] = blank
                ref[z, x, top : top + 8, :] = blank
        return carry

    lax.fori_loop(0, 10, clear, 0)
    for ref in (one, two):
        for z in (0, 9):
            for x in range(columns):
                ref[z, x, 8:top, :] = jnp.zeros((height + 8, LANES), F32)

    def place(u_row, c_row, tile):
        for x in range(columns):
            for z in range(8):
                one[1 + z, x, 8 + tile : 16 + tile, :] = blank
                coef_a[z, x, tile : tile + 8, :] = blank
                coef_b[z, x, tile : tile + 8, :] = blank
                coef_k[z, x, tile : tile + 8, :] = blank
        for x, span in enumerate(spans):
            for i in range(4):
                one[1:9, x, u_row + i, :] = got_ref[i, :, span]
            for i in range(3):
                k = DT * got_ref[4 + i, :, span]
                g = DT * got_ref[7 + i, :, span]
                coef_k[:, x, c_row + i, :] = k
                coef_b[:, x, c_row + i, :] = g * (1.0 / 3.0)
                coef_a[:, x, c_row + i, :] = 1.0 + (g - 6.0 * k)

    @pl.when(above)
    def _():
        place(8 + height, height, height)

    @pl.when(jnp.logical_not(above))
    def _():
        place(12, 5, 0)

    k_copy.wait()
    g_copy.wait()

    def widen(z, carry):
        for x, span in enumerate(spans):
            for r in range(0, height, 16):
                k = DT * k_nat[z, r : r + 16, span].astype(F32)
                g = DT * g_nat[z, r : r + 16, span].astype(F32)
                rows = pl.ds(own + r, 16)
                coef_k[z, x, rows, :] = k
                coef_b[z, x, rows, :] = g * (1.0 / 3.0)
                coef_a[z, x, rows, :] = 1.0 + (g - 6.0 * k)
        return carry

    lax.fori_loop(0, 8, widen, 0)
    for copy in copies:
        copy.wait()

    lane = lax.broadcasted_iota(jnp.int32, (8, LANES), 1)
    first, final = lane == 0, lane == LANES - 1

    def sweep(source, target, level, shift):
        def body(z, carry):
            for row in range(8, top, 8):
                tiles = [source[z + 1, x, row : row + 8, :] for x in range(columns)]
                back = [pltpu.roll(t, LANES - 1, 1) for t in tiles] + [blank]
                forth = [blank] + [pltpu.roll(t, 1, 1) for t in tiles]
                for x, u in enumerate(tiles):
                    x_next = jnp.where(final, back[x + 1], back[x])
                    x_prev = jnp.where(first, forth[x], forth[x + 1])
                    plus = source[z + 1, x, row + 1 : row + 9, :] + x_next
                    minus = source[z + 1, x, row - 1 : row + 7, :] + x_prev
                    levels = source[z, x, row : row + 8, :] + source[z + 2, x, row : row + 8, :]
                    rows = slice(row - 8, row)
                    own_part = u * (coef_a[z, x, rows, :] - coef_b[z, x, rows, :] * (u * u))
                    spread = coef_k[z, x, rows, :] * ((plus + minus) + levels)
                    out = (own_part + spread) - (0.5 * VEL * DT) * (plus - minus)
                    if shift is None:
                        target[z + level, x, row : row + 8, :] = out
                    else:
                        target[z + level, x, pl.ds(pl.multiple_of(row + shift, 8), 8), :] = out
            return carry

        lax.fori_loop(0, 8, body, 0, unroll=8)

    def keep(step, source):
        def write(row):
            for x, span in enumerate(spans):
                for i in range(2):
                    steps_ref[2 * step + i, :, span] = source[1:9, x, row + i, :]

        @pl.when(above)
        def _():
            write(8 + step)

        @pl.when(jnp.logical_not(above))
        def _():
            write(16 + height - 2 - step)

    def keep_coefs(row):
        for x, span in enumerate(spans):
            for i in range(4):
                coefs_ref[0, i, :, span] = coef_a[:, x, row + i, :]
                coefs_ref[1, i, :, span] = coef_b[:, x, row + i, :]
                coefs_ref[2, i, :, span] = coef_k[:, x, row + i, :]

    @pl.when(above)
    def _():
        keep_coefs(0)

    @pl.when(jnp.logical_not(above))
    def _():
        keep_coefs(8 + height - 4)

    pool = pool_matrix(breadth, 1.0 / 16.0)

    def sums_of(ref, level, start, part):
        def body(z, carry):
            for x, span in enumerate(spans):
                parts = [ref[z + level, x, pl.ds(start + i, small, stride=4), :] for i in range(4)]
                flat[part, z, :, span] = (parts[0] + parts[1]) + (parts[2] + parts[3])
            return carry

        lax.fori_loop(0, 8, body, 0, unroll=2)

    def pooled_into(targets, scales):
        count = len(targets)
        means = split_dot(flat[0:count].reshape(count * 8 * small, breadth), pool).reshape(count, 8, small, thin)
        for part in range(count):
            flat[part, :, :, 0:thin] = means[part] * scales[part]
            for r in range(small):
                targets[part][r] = flat[part, :, r, 0:thin]

    sums_of(one, 1, 8 + own, 0)
    sums_of(coef_k, 0, own, 1)
    sums_of(coef_b, 0, own, 2)
    pooled_into([coarse_ref.at[0], coarse_ref.at[1], coarse_ref.at[2]], (1.0, 2.0, 6.0))
    keep(0, one)
    sweep(one, two, 1, None)
    keep(1, two)
    sweep(two, one, 1, None)
    keep(2, one)
    sweep(one, two, 1, None)
    keep(3, two)
    sweep(two, fine_ref, 0, jnp.where(above, 0, -8))
    sums_of(fine_ref, 0, 8, 0)
    pooled_into([end_ref], (1.0,))


def inner(starts, diffusivity, reaction, got):
    height, breadth = starts.shape[2:]
    small = height // 4
    columns = breadth // LANES
    wide = pltpu.VMEM((10, columns, height + 24, LANES), F32)
    coef = pltpu.VMEM((8, columns, height + 8, LANES), F32)
    return pl.pallas_call(
        inner_kernel,
        out_shape=[
            struct(8, columns, height + 16, LANES),
            struct(8, 8, breadth),
            struct(3, 4, 8, breadth),
            struct(3, small, 8, breadth // 4),
            struct(small, 8, breadth // 4),
        ],
        in_specs=[ANY] * 3 + [VMEM],
        out_specs=[VMEM] * 5,
        scratch_shapes=[wide, wide, coef, coef, coef]
        + [
            pltpu.VMEM((8, height, breadth), BF16),
            pltpu.VMEM((8, height, breadth), BF16),
            pltpu.VMEM((3, 8, small, breadth), F32),
            pltpu.SemaphoreType.DMA((columns + 2,)),
        ],
        compiler_params=params(28),
        cost_estimate=pl.CostEstimate(flops=30_000_000, bytes_accessed=4_000_000, transcendentals=0),
        name="inner_updates",
    )(starts, diffusivity, reaction, got)


def rows_for(array, low_side, reach):
    start = jnp.where(low_side, 0, array.shape[1] - reach)
    return lax.dynamic_slice_in_dim(array, start, reach, axis=1)


def even_pairs():
    return [(i, i ^ 1) for i in range(lax.axis_size("space"))]


def swap_odd(block):
    places = lax.axis_size("space")
    slices = lax.axis_size("tm")

    def partner(time, place):
        if 0 < place < places - 1 or slices % 2:
            return time, (place - 1 if place % 2 == 0 else place + 1) % places
        return time ^ 1, place

    pairs = []
    for time in range(slices):
        for place in range(places):
            other, near = partner(time, place)
            pairs.append((time * places + place, other * places + near))
    return lax.ppermute(block, ("tm", "space"), pairs)


def alive():
    place = lax.axis_index("space")
    last = lax.axis_size("space") - 1
    return jnp.where(jnp.logical_or(place == 0, place == last), 0.0, 1.0).astype(F32)


def edge_kernel(
    steps_ref, coefs_ref, got_ref, even_ref, end_in, coarse_ref, rows_ref, end_ref, jump_ref,
    zero, one, two, three, coef_a, coef_b, coef_k, seen, half, coarse_k, coarse_g,
):
    breadth = got_ref.shape[2]
    small = end_ref.shape[0]
    low_side = parity() == 0
    live = alive()
    edges = masks()
    states = (zero, one, two, three, rows_ref)

    def index(distance):
        return jnp.where(low_side, 4 + distance, 7 - distance)

    for i in range(4):
        coef_a[4 + i] = coefs_ref[0, i]
        coef_b[4 + i] = coefs_ref[1, i]
        coef_k[4 + i] = coefs_ref[2, i]
    set_coefs(got_ref[4], got_ref[5], coef_a, coef_b, coef_k, index(-1))
    zero[index(-1)] = got_ref[0] * live
    one[index(-2)] = got_ref[2] * live
    for step in range(4):
        at = jnp.where(low_side, 4 + step, 6 - step)
        for i in range(2):
            states[step][at + i] = steps_ref[2 * step + i]
    toward = jnp.where(low_side, -0.5 * VEL * DT, 0.5 * VEL * DT)
    one[index(-1)] = (got_ref[1] + (DT * got_ref[4] + toward) * zero[index(0)]) * live
    two[index(-2)] = (got_ref[3] + (DT * got_ref[6] + toward) * one[index(-1)]) * live
    for step in range(1, 5):
        for distance in range(0 if step in (1, 4) else -1, step):
            at = index(distance)
            tiles = fine_row(states[step - 1], at, coef_a, coef_b, coef_k, at, breadth, edges)
            if distance < 0:
                tiles = [t * live for t in tiles]
            put_tiles(states[step], at - 4 if step == 4 else at, tiles)
    pool = pool_matrix(breadth, 1.0 / 16.0)
    end_ref[...] = end_in[...]
    end_ref[jnp.where(low_side, 0, small - 1)] = pooled(rows_ref, 0, 1, pool)

    thin = breadth // 4
    odd_at = jnp.where(low_side, 0, 2 + small)
    even_at = jnp.where(low_side, 2 + small, 0)
    near = jnp.where(low_side, 1, 2 + small)
    far = jnp.where(low_side, 2 + small, 1)
    for r in range(small):
        seen[2 + r] = coarse_ref[0, r]
        coarse_k[2 + r] = coarse_ref[1, r]
        coarse_g[2 + r] = coarse_ref[2, r]
    for i in range(2):
        span = slice(i * thin, (i + 1) * thin)
        seen[odd_at + i] = got_ref[7, :, span] * live
        seen[even_at + i] = even_ref[10, :, span]
    for i, ref in ((2, coarse_k), (3, coarse_g)):
        span = slice(i * thin, (i + 1) * thin)
        ref[near] = got_ref[7, :, span]
        ref[far] = even_ref[10, :, span]
    coarse_sweep(seen, half, coarse_k, coarse_g, 1, small + 3, 2, small, low_side, live, edges)
    first = lax.axis_index("tm") == 0
    for r in range(small):
        tiles = coarse_row(half, 2 + r, coarse_k, coarse_g, 2 + r, thin, edges)
        for i, tile in enumerate(tiles):
            span = slice(i * LANES, (i + 1) * LANES)
            jump_ref[r, :, span] = end_ref[r, :, span] - jnp.where(first, 0.0, tile)


def fill_coarse(wide, own, even_part, odd_part, reach, low_side, live):
    rows = own.shape[0]
    count = even_part.shape[0]
    for r in range(rows):
        wide[reach + r] = own[r]
    odd_at = jnp.where(low_side, 0, reach + rows)
    even_at = jnp.where(low_side, reach + rows, 0)
    odd_from = jnp.where(low_side, count - reach, 0)
    even_from = jnp.where(low_side, 0, count - reach)
    for i in range(reach):
        wide[odd_at + i] = odd_part[odd_from + i] * live
        wide[even_at + i] = even_part[even_from + i]


def coarse_sweep(source, target, coef_k, coef_g, low, high, reach, rows, low_side, live, edges, shift=0):
    breadth = source.shape[2]
    for row in range(low, high):
        tiles = coarse_row(source, row, coef_k, coef_g, row + shift, breadth, edges)
        if row < reach:
            factor = jnp.where(low_side, live, 1.0)
            tiles = [t * factor for t in tiles]
        elif row >= reach + rows:
            factor = jnp.where(low_side, 1.0, live)
            tiles = [t * factor for t in tiles]
        put_tiles(target, row, tiles)


def edge(steps, coefs, got, even_got, end, coarse):
    breadth = got.shape[2]
    small = end.shape[0]
    wide = pltpu.VMEM((12, 8, breadth), F32)
    thin = pltpu.VMEM((small + 4, 8, breadth // 4), F32)
    return pl.pallas_call(
        edge_kernel,
        out_shape=[
            struct(4, 8, breadth),
            struct(small, 8, breadth // 4),
            struct(small, 8, breadth // 4),
        ],
        in_specs=[VMEM] * 6,
        out_specs=[VMEM] * 3,
        scratch_shapes=[wide] * 7 + [thin] * 4,
        compiler_params=params(16),
        name="edge_updates",
    )(steps, coefs, got, even_got, end, coarse)


def last_kernel(behind, *refs):
    before, refs = refs[:behind], refs[behind:]
    fine_hbm, rows_ref, end_ref, jump_ref, even_j, odd_j, coarse_ref, even_c, odd_c, out_hbm = refs[:10]
    fine_ref, out_ref, one, two, coarse_k, coarse_g, added, change, moved, sems = refs[10:]
    reach = COARSE * behind
    height, breadth = out_hbm.shape[2:]
    columns = breadth // LANES
    small = height // 4
    fetch = pltpu.make_async_copy(fine_hbm, fine_ref, sems.at[8])
    fetch.start()
    low_side = parity() == 0
    live = alive()
    edges = masks()
    slice_id = lax.axis_index("tm")
    fill_coarse(coarse_k, coarse_ref.at[1], even_c.at[0], odd_c.at[0], reach, low_side, live)
    fill_coarse(coarse_g, coarse_ref.at[2], even_c.at[1], odd_c.at[1], reach, low_side, live)
    at = 0
    for j in range(behind):
        width = reach - COARSE * j
        ok = jnp.where(slice_id >= behind - j, 1.0, 0.0).astype(F32)
        target = one if j == 0 else added
        base = reach - width
        for r in range(small):
            target[reach + r] = before[j][r] * ok
        odd_at = jnp.where(low_side, base, reach + small)
        even_at = jnp.where(low_side, reach + small, base)
        for i in range(width):
            target[odd_at + i] = odd_j[at + i] * (ok * live)
            target[even_at + i] = even_j[at + i] * ok
        at += width
        if j > 0:
            for r in range(base, reach + small + width):
                one[r] = one[r] + added[r]
        coarse_sweep(one, two, coarse_k, coarse_g, base + 1, reach + small + width - 1, reach, small, low_side, live, edges)
        coarse_sweep(two, one, coarse_k, coarse_g, base + 2, reach + small + width - 2, reach, small, low_side, live, edges)
    for r in range(small):
        change[:, r, :] = (one[reach + r] + jump_ref[r]) - end_ref[r]
    spread = spread_matrix(breadth)
    moved[...] = split_dot(change[...].reshape(8 * small, breadth // 4), spread).reshape(8, small, breadth)
    fetch.wait()

    def fix(row):
        for x in range(columns):
            for i in range(4):
                fine_ref[:, x, row + i, :] = rows_ref[i, :, x * LANES : (x + 1) * LANES]

    @pl.when(low_side)
    def _():
        fix(8)

    @pl.when(jnp.logical_not(low_side))
    def _():
        fix(8 + height - 4)

    lower = lax.broadcasted_iota(jnp.int32, (8, LANES), 0) < 4

    def body(z, carry):
        for x in range(columns):
            span = slice(x * LANES, (x + 1) * LANES)
            for row in range(0, height, 8):
                c = row // 4
                step = jnp.where(lower, moved[z, c : c + 1, span], moved[z, c + 1 : c + 2, span])
                out_ref[z, row : row + 8, span] = fine_ref[z, x, 8 + row : 16 + row, :] + step
        pltpu.make_async_copy(out_ref.at[z], out_hbm.at[0, z], sems.at[z]).start()
        return carry

    lax.fori_loop(0, 8, body, 0)
    for z in range(8):
        pltpu.make_async_copy(out_ref.at[z], out_hbm.at[0, z], sems.at[z]).wait()


def last(fine, rows, end, jump, before, even_j, odd_j, coarse, even_c, odd_c, height):
    breadth = rows.shape[2]
    small = height // 4
    reach = COARSE * len(before)
    thin = pltpu.VMEM((small + 2 * reach, 8, breadth // 4), F32)
    return pl.pallas_call(
        functools.partial(last_kernel, len(before)),
        out_shape=struct(1, 8, height, breadth),
        in_specs=[VMEM] * len(before) + [ANY] + [VMEM] * 8,
        out_specs=HBM,
        scratch_shapes=[pltpu.VMEM(fine.shape, F32), pltpu.VMEM((8, height, breadth), F32)]
        + [thin] * 5
        + [
            pltpu.VMEM((8, small, breadth // 4), F32),
            pltpu.VMEM((8, small, breadth), F32),
            pltpu.SemaphoreType.DMA((9,)),
        ],
        compiler_params=params(16),
        name="chain_and_spread",
    )(*before, fine, rows, end, jump, even_j, odd_j, coarse, even_c, odd_c)


def relay(jump, coarse, even_c, odd_c, even):
    low_side = parity() == 0
    live = alive()
    small = jump.shape[0]

    def widened(own, even_part, odd_part):
        odd_part = odd_part * live
        low = jnp.where(low_side, odd_part, even_part)
        high = jnp.where(low_side, even_part, odd_part)
        return jnp.concatenate([low, own, high], axis=1)

    def update(values, k, g):
        rows = values.shape[0] - 2
        middle = values[1:-1]
        plus = values[2:] + jnp.pad(middle, ((0, 0), (0, 0), (0, 1)))[:, :, 1:]
        minus = values[:-2] + jnp.pad(middle, ((0, 0), (0, 0), (1, 0)))[:, :, :-1]
        levels = jnp.pad(middle, ((0, 0), (0, 1), (0, 0)))[:, 1:] + jnp.pad(middle, ((0, 0), (1, 0), (0, 0)))[:, :-1]
        bend = levels - 2.0 * middle + (plus + minus - 4.0 * middle) / 16.0
        drift = VEL * (plus - minus) / 8.0
        return middle + (k * bend - 2.0 * DT * drift + g * (middle - middle * middle * middle / 3.0))

    coefs = widened(coarse[1:], even_c, odd_c)
    place = lax.axis_index("space")
    start = jnp.where(place == 0, 1, 0)
    stop = jnp.where(place == lax.axis_size("space") - 1, small + 1, small + 2)
    row = jnp.arange(small + 2)[:, None, None]
    inside = jnp.logical_and(row >= start, row < stop)

    def advance(values):
        block = values[None]
        even_v = lax.ppermute(rows_for(block, jnp.logical_not(low_side), 2), "space", even)
        odd_v = swap_odd(rows_for(block, low_side, 2))
        wide = widened(block, even_v, odd_v)[0]
        wide = jnp.where(inside, update(wide, coefs[0, 1:-1], coefs[1, 1:-1]), 0.0)
        return update(wide, coarse[1], coarse[2])

    slice_id = lax.axis_index("tm")
    slices = lax.axis_size("tm")
    onward = [(i, i + 1) for i in range(slices - 1)]

    def link(position, state):
        incoming = lax.ppermute(state, "tm", onward)
        return jnp.where(slice_id > 0, advance(incoming), 0.0) + jump

    return lax.fori_loop(0, slices - 1, link, jump)


def per_device(starts, diffusivity, reaction):
    height, breadth = starts.shape[2:]
    small = height // 4
    slices = lax.axis_size("tm")
    behind = slices - 1
    reach = COARSE * behind
    at_once = 0 < behind and reach <= small
    even = even_pairs()
    low_side = parity() == 0
    high_side = jnp.logical_not(low_side)

    odd_rows = odd_pack(starts, diffusivity, reaction)
    odd_got = swap_odd(odd_rows)
    even_got = lax.ppermute(even_pack(odd_rows, starts, diffusivity, reaction), "space", even)
    fine, steps, coefs, coarse, end = inner(starts, diffusivity, reaction, even_got)
    rows, end, jump = edge(steps, coefs, odd_got, even_got, end, coarse)
    width = reach if at_once else COARSE
    later, jump = lax.optimization_barrier((coarse[1:], jump))
    odd_c = swap_odd(rows_for(later, low_side, width))
    even_c = lax.ppermute(rows_for(later, high_side, width), "space", even)
    if at_once:
        before = [
            lax.ppermute(jump, "tm", [(i, (i + k) % slices) for i in range(slices)])
            for k in range(behind, 0, -1)
        ]

        def outer(low):
            return jnp.concatenate(
                [rows_for(before[j][None], low, reach - COARSE * j)[0] for j in range(behind)], axis=0
            )

        odd_j = swap_odd(outer(low_side))
        even_j = lax.ppermute(outer(high_side), "space", even)
        return last(fine, rows, end, jump, before, even_j, odd_j, coarse, even_c, odd_c, height)
    chained = relay(jump, coarse, even_c, odd_c, even)
    change = jnp.repeat(jnp.repeat(jnp.transpose(chained - end, (1, 0, 2)), 4, axis=1), 4, axis=2)
    fixed = jnp.where(low_side, 0, height - 4)
    fine = jnp.transpose(fine[:, :, 8 : 8 + height], (0, 2, 1, 3)).reshape(8, height, breadth)
    fine = lax.dynamic_update_slice_in_dim(fine, jnp.transpose(rows, (1, 0, 2)), fixed, axis=1)
    return (fine + change)[None]


def solution(mesh):
    in_specs = (P("tm", None, "space", None), P(None, "space", None), P(None, "space", None))
    out_specs = P("tm", None, "space", None)
    return jax.shard_map(per_device, mesh=mesh, in_specs=in_specs, out_specs=out_specs, check_vma=False)
```

```python
import functools

import jax
import jax.numpy as jnp
from jax import lax
from jax.experimental import pallas as pl
from jax.experimental.pallas import tpu as pltpu
from jax.sharding import PartitionSpec as P

FINE = 4
COARSE = 2
DT = 0.05
VEL = 0.5
LANES = 128
F32 = jnp.float32
BF16 = jnp.bfloat16
ODD_MIB = 53.4

VMEM = pl.BlockSpec(memory_space=pltpu.VMEM)
ANY = pl.BlockSpec(memory_space=pl.ANY)
HBM = pl.BlockSpec(memory_space=pltpu.HBM)


def params(mib):
    return pltpu.CompilerParams(vmem_limit_bytes=int(mib * 2**20))


def struct(*shape):
    return jax.ShapeDtypeStruct(shape, F32)


def parity():
    return lax.rem(lax.axis_index("space"), 2)


def tiles_of(ref, row, breadth):
    return [ref[row, :, i : i + LANES] for i in range(0, breadth, LANES)]


def put_tiles(ref, row, tiles):
    for i, tile in enumerate(tiles):
        ref[row, :, i * LANES : (i + 1) * LANES] = tile


def masks():
    lane = lax.broadcasted_iota(jnp.int32, (8, LANES), 1)
    level = lax.broadcasted_iota(jnp.int32, (8, LANES), 0)
    return lane == 0, lane == LANES - 1, level == 0, level == 7


def neighbours(tiles, edges):
    first, last, bottom, top = edges
    back = [pltpu.roll(t, LANES - 1, 1) for t in tiles]
    forth = [pltpu.roll(t, 1, 1) for t in tiles]
    zero = jnp.zeros_like(tiles[0])
    x_next = [jnp.where(last, b, a) for a, b in zip(back, back[1:] + [zero])]
    x_prev = [jnp.where(first, b, a) for a, b in zip(forth, [zero] + forth[:-1])]
    levels = [
        jnp.where(top, 0.0, pltpu.roll(t, 7, 0)) + jnp.where(bottom, 0.0, pltpu.roll(t, 1, 0))
        for t in tiles
    ]
    return x_next, x_prev, levels


def fine_row(state, row, coef_a, coef_b, coef_k, coef_row, breadth, edges):
    tiles = tiles_of(state, row, breadth)
    x_next, x_prev, levels = neighbours(tiles, edges)
    out = []
    for i, u in enumerate(tiles):
        span = slice(i * LANES, (i + 1) * LANES)
        plus = state[row + 1, :, span] + x_next[i]
        minus = state[row - 1, :, span] + x_prev[i]
        own = u * (coef_a[coef_row, :, span] - coef_b[coef_row, :, span] * (u * u))
        spread = coef_k[coef_row, :, span] * ((plus + minus) + levels[i])
        out.append((own + spread) - (0.5 * VEL * DT) * (plus - minus))
    return out


def coarse_row(state, row, coef_k, coef_g, coef_row, breadth, edges):
    tiles = tiles_of(state, row, breadth)
    x_next, x_prev, levels = neighbours(tiles, edges)
    out = []
    for i, c in enumerate(tiles):
        span = slice(i * LANES, (i + 1) * LANES)
        plus = state[row + 1, :, span] + x_next[i]
        minus = state[row - 1, :, span] + x_prev[i]
        k = coef_k[coef_row, :, span]
        g = coef_g[coef_row, :, span]
        bend = (levels[i] - 2.0 * c) + ((plus + minus) - 4.0 * c) * (1.0 / 16.0)
        drift = (2.0 * DT * VEL / 8.0) * (plus - minus)
        out.append(c + ((k * bend - drift) + g * (c - c * c * c * (1.0 / 3.0))))
    return out


def split_dot(values, matrix):
    high = values.astype(BF16)
    low = (values - high.astype(F32)).astype(BF16)
    both = jnp.dot(jnp.concatenate([high, low], axis=0), matrix, preferred_element_type=F32)
    rows = values.shape[0]
    return both[:rows] + both[rows:]


def pool_matrix(breadth, value):
    fine = lax.broadcasted_iota(jnp.int32, (breadth, breadth // 4), 0)
    coarse = lax.broadcasted_iota(jnp.int32, (breadth, breadth // 4), 1)
    return jnp.where(fine // 4 == coarse, value, 0.0).astype(BF16)


def spread_matrix(breadth):
    coarse = lax.broadcasted_iota(jnp.int32, (breadth // 4, breadth), 0)
    fine = lax.broadcasted_iota(jnp.int32, (breadth // 4, breadth), 1)
    return jnp.where(fine // 4 == coarse, 1.0, 0.0).astype(BF16)


def pooled(ref, first_row, coarse_rows, pool):
    sums = []
    for c in range(coarse_rows):
        r = first_row + 4 * c
        sums.append((ref[r] + ref[r + 1]) + (ref[r + 2] + ref[r + 3]))
    return split_dot(jnp.concatenate(sums, axis=0), pool)


def set_coefs(k, g, a_ref, b_ref, k_ref, row):
    k = DT * k
    g = DT * g
    k_ref[row] = k
    b_ref[row] = g * (1.0 / 3.0)
    a_ref[row] = 1.0 + (g - 6.0 * k)


def put_pooled(ref, row, sums, pool):
    thin = ref.shape[2] // 4
    small = split_dot(jnp.concatenate(sums, axis=0), pool)
    for i in range(4):
        value = small[8 * i : 8 * i + 8] * (1.0 if i < 2 else 2.0 * DT)
        ref[row, :, i * thin : (i + 1) * thin] = value


def sums_of_four(*arrays):
    return [(r[0] + r[1]) + (r[2] + r[3]) for r in arrays]


def message(high, u_rows, k_rows, g_rows, ref, last_ref, last_row, state, after, coefs, pool, edges):
    breadth = ref.shape[2]
    near = 4 if high else 1
    step = -1 if high else 1
    zeros = jnp.zeros((8, breadth), F32)
    state[0] = zeros
    state[5] = zeros
    after[0] = zeros
    after[3] = zeros
    for i in range(4):
        state[1 + i] = u_rows[(4 if high else 0) + i]
        set_coefs(k_rows[i], g_rows[i], *coefs, 1 + i)
    ref[0] = state[near]
    put_tiles(ref, 1, fine_row(state, near, *coefs, near, breadth, edges))
    one = fine_row(state, near + step, *coefs, near + step, breadth, edges)
    two = fine_row(state, near + 2 * step, *coefs, near + 2 * step, breadth, edges)
    put_tiles(ref, 2, one)
    place = 2 if high else 1
    put_tiles(after, place, one)
    put_tiles(after, place + step, two)
    put_tiles(ref, 3, fine_row(after, place, *coefs, near + step, breadth, edges))
    ref[4] = k_rows[near - 1]
    ref[5] = g_rows[near - 1]
    ref[6] = k_rows[near - 1 + step]
    put_pooled(last_ref, last_row, sums_of_four(u_rows[:4], u_rows[4:], k_rows, g_rows), pool)


def odd_kernel(
    u_hbm, k_hbm, g_hbm, odd_ref, u_nat, k_nat, g_nat, k_wide, g_wide, state, after, coef_a, coef_b, coef_k, sems
):
    height, breadth = u_hbm.shape[2:]
    low_side = parity() == 0
    row8 = pl.multiple_of(jnp.where(low_side, 0, height - 8), 8)
    row16 = pl.multiple_of(jnp.where(low_side, 0, height - 16), 16)
    copies = [
        pltpu.make_async_copy(u_hbm.at[0, :, pl.ds(row8, 8), :], u_nat, sems.at[0]),
        pltpu.make_async_copy(k_hbm.at[:, pl.ds(row16, 16), :], k_nat, sems.at[1]),
        pltpu.make_async_copy(g_hbm.at[:, pl.ds(row16, 16), :], g_nat, sems.at[2]),
    ]
    for copy in copies:
        copy.start()
    pool = pool_matrix(breadth, 1.0 / 16.0)
    edges = masks()
    for copy in copies:
        copy.wait()
    k_wide[...] = k_nat[...].astype(F32)
    g_wide[...] = g_nat[...].astype(F32)

    def fill(high):
        low = 12 if high else 0
        u_rows = [u_nat[:, i, :] for i in range(8)]
        k_rows = [k_wide[:, low + i, :] for i in range(4)]
        g_rows = [g_wide[:, low + i, :] for i in range(4)]
        coefs = (coef_a, coef_b, coef_k)
        message(high, u_rows, k_rows, g_rows, odd_ref, odd_ref, 7, state, after, coefs, pool, edges)

    @pl.when(low_side)
    def _():
        fill(0)

    @pl.when(jnp.logical_not(low_side))
    def _():
        fill(1)


def odd_pack(starts, diffusivity, reaction):
    breadth = starts.shape[3]
    coef = pltpu.VMEM((6, 8, breadth), F32)
    return pl.pallas_call(
        odd_kernel,
        out_shape=struct(8, 8, breadth),
        in_specs=[HBM] * 3,
        out_specs=VMEM,
        scratch_shapes=[
            pltpu.VMEM((8, 8, breadth), F32),
            pltpu.VMEM((8, 16, breadth), BF16),
            pltpu.VMEM((8, 16, breadth), BF16),
            pltpu.VMEM((8, 16, breadth), F32),
            pltpu.VMEM((8, 16, breadth), F32),
            coef,
            pltpu.VMEM((4, 8, breadth), F32),
            coef,
            coef,
            coef,
            pltpu.SemaphoreType.DMA((3,)),
        ],
        compiler_params=params(ODD_MIB),
        name="odd_rows",
    )(starts, diffusivity, reaction)


def side_rows(high, u_ref, k_ref, g_ref, k_wide, g_wide):
    height = u_ref.shape[2]
    k_wide[...] = k_ref[:, height - 16 if high else 0 : height if high else 16, :].astype(F32)
    g_wide[...] = g_ref[:, height - 16 if high else 0 : height if high else 16, :].astype(F32)
    low = 12 if high else 0
    u_rows = [u_ref[0, :, (height - 8 if high else 0) + i, :] for i in range(8)]
    k_rows = [k_wide[:, low + i, :] for i in range(4)]
    g_rows = [g_wide[:, low + i, :] for i in range(4)]
    return u_rows, k_rows, g_rows


def even_kernel(odd_rows, u_ref, k_ref, g_ref, even_ref, rest_ref, k_wide, g_wide, state, after, coef_a, coef_b, coef_k):
    del odd_rows
    pool = pool_matrix(u_ref.shape[3], 1.0 / 16.0)
    edges = masks()

    def fill(high):
        coefs = (coef_a, coef_b, coef_k)
        rows = side_rows(high, u_ref, k_ref, g_ref, k_wide, g_wide)
        message(high, *rows, even_ref, rest_ref, 0, state, after, coefs, pool, edges)

    above = parity() == 0

    @pl.when(above)
    def _():
        fill(1)

    @pl.when(jnp.logical_not(above))
    def _():
        fill(0)


def even_pack(odd_rows, starts, diffusivity, reaction):
    breadth = starts.shape[3]
    coef = pltpu.VMEM((6, 8, breadth), F32)
    return pl.pallas_call(
        even_kernel,
        out_shape=[struct(7, 8, breadth), struct(1, 8, breadth)],
        in_specs=[ANY] + [VMEM] * 3,
        out_specs=[VMEM] * 2,
        scratch_shapes=[pltpu.VMEM((8, 16, breadth), F32)] * 2
        + [coef, pltpu.VMEM((4, 8, breadth), F32), coef, coef, coef],
        compiler_params=params(16),
        name="even_rows",
    )(odd_rows, starts, diffusivity, reaction)


def pooled_into(flat, targets, scales, pool):
    count = len(targets)
    _, _, small, breadth = flat.shape
    thin = breadth // 4
    means = split_dot(flat[0:count].reshape(count * 8 * small, breadth), pool).reshape(count, 8, small, thin)
    for part in range(count):
        flat[part, :, :, 0:thin] = means[part] * scales[part]
        for r in range(small):
            targets[part][r] = flat[part, :, r, 0:thin]


def sums_of(ref, level, start, flat, part):
    small = flat.shape[2]

    def body(z, carry):
        for x in range(ref.shape[1]):
            rows = [ref[z + level, x, pl.ds(start + i, small, stride=4), :] for i in range(4)]
            flat[part, z, :, x * LANES : (x + 1) * LANES] = (rows[0] + rows[1]) + (rows[2] + rows[3])
        return carry

    lax.fori_loop(0, 8, body, 0, unroll=2)


def clear_ends(ref, top):
    blank = jnp.zeros((8, LANES), F32)
    columns = ref.shape[1]

    def clear(z, carry):
        for x in range(columns):
            ref[z, x, 0:8, :] = blank
            ref[z, x, top : top + 8, :] = blank
        return carry

    lax.fori_loop(0, 10, clear, 0)
    for z in (0, 9):
        for x in range(columns):
            ref[z, x, 8:top, :] = jnp.zeros((top - 8, LANES), F32)


def inner_kernel(
    u_hbm, k_hbm, g_hbm, fine_ref, low_ref, high_ref, coarse_ref, end_ref,
    one, two, coef_a, coef_b, coef_k, k_nat, g_nat, flat, sems,
):
    height, breadth = u_hbm.shape[2:]
    columns = breadth // LANES
    spans = [slice(x * LANES, (x + 1) * LANES) for x in range(columns)]
    top = height + 8
    copies = [
        pltpu.make_async_copy(
            u_hbm.at[0, :, :, pl.ds(x * LANES, LANES)], one.at[pl.ds(1, 8), x, pl.ds(8, height), :], sems.at[x]
        )
        for x in range(columns)
    ]
    k_copy = pltpu.make_async_copy(k_hbm, k_nat, sems.at[columns])
    g_copy = pltpu.make_async_copy(g_hbm, g_nat, sems.at[columns + 1])
    for copy in [k_copy, g_copy] + copies:
        copy.start()
    clear_ends(one, top)
    clear_ends(two, top)
    pool = pool_matrix(breadth, 1.0 / 16.0)
    k_copy.wait()
    g_copy.wait()

    def widen(z, carry):
        for x, span in enumerate(spans):
            for r in range(0, height, 16):
                k = DT * k_nat[z, r : r + 16, span].astype(F32)
                g = DT * g_nat[z, r : r + 16, span].astype(F32)
                coef_k[z, x, r : r + 16, :] = k
                coef_b[z, x, r : r + 16, :] = g * (1.0 / 3.0)
                coef_a[z, x, r : r + 16, :] = 1.0 + (g - 6.0 * k)
        return carry

    lax.fori_loop(0, 8, widen, 0)
    for copy in copies:
        copy.wait()
    sums_of(one, 1, 8, flat, 0)
    sums_of(coef_k, 0, 0, flat, 1)
    sums_of(coef_b, 0, 0, flat, 2)
    pooled_into(flat, [coarse_ref.at[0], coarse_ref.at[1], coarse_ref.at[2]], (1.0, 2.0, 6.0), pool)

    lane = lax.broadcasted_iota(jnp.int32, (8, LANES), 1)
    first, final = lane == 0, lane == LANES - 1
    blank = jnp.zeros((8, LANES), F32)

    def sweep(source, target, level, shift):
        def body(z, carry):
            for row in range(8, top, 8):
                tiles = [source[z + 1, x, row : row + 8, :] for x in range(columns)]
                back = [pltpu.roll(t, LANES - 1, 1) for t in tiles] + [blank]
                forth = [blank] + [pltpu.roll(t, 1, 1) for t in tiles]
                for x, u in enumerate(tiles):
                    x_next = jnp.where(final, back[x + 1], back[x])
                    x_prev = jnp.where(first, forth[x], forth[x + 1])
                    plus = source[z + 1, x, row + 1 : row + 9, :] + x_next
                    minus = source[z + 1, x, row - 1 : row + 7, :] + x_prev
                    levels = source[z, x, row : row + 8, :] + source[z + 2, x, row : row + 8, :]
                    rows = slice(row - 8, row)
                    own_part = u * (coef_a[z, x, rows, :] - coef_b[z, x, rows, :] * (u * u))
                    spread = coef_k[z, x, rows, :] * ((plus + minus) + levels)
                    out = (own_part + spread) - (0.5 * VEL * DT) * (plus - minus)
                    target[z + level, x, row + shift : row + shift + 8, :] = out
            return carry

        lax.fori_loop(0, 8, body, 0, unroll=8)

    def keep(step, source):
        for x, span in enumerate(spans):
            for i in range(2):
                low_ref[2 * step - 2 + i, :, span] = source[1:9, x, 8 + step + i, :]
                high_ref[2 * step - 2 + i, :, span] = source[1:9, x, top - 2 - step + i, :]

    sweep(one, two, 1, 0)
    keep(1, two)
    sweep(two, one, 1, 0)
    keep(2, one)
    sweep(one, two, 1, 0)
    keep(3, two)
    sweep(two, fine_ref, 0, -8)
    sums_of(fine_ref, 0, 0, flat, 0)
    pooled_into(flat, [end_ref], (1.0,), pool)


def inner(starts, diffusivity, reaction):
    height, breadth = starts.shape[2:]
    small = height // 4
    columns = breadth // LANES
    wide = pltpu.VMEM((10, columns, height + 16, LANES), F32)
    coef = pltpu.VMEM((8, columns, height, LANES), F32)
    return pl.pallas_call(
        inner_kernel,
        out_shape=[
            struct(8, columns, height, LANES),
            struct(6, 8, breadth),
            struct(6, 8, breadth),
            struct(3, small, 8, breadth // 4),
            struct(small, 8, breadth // 4),
        ],
        in_specs=[ANY] * 3,
        out_specs=[VMEM] * 5,
        scratch_shapes=[wide, wide, coef, coef, coef]
        + [
            pltpu.VMEM((8, height, breadth), BF16),
            pltpu.VMEM((8, height, breadth), BF16),
            pltpu.VMEM((3, 8, small, breadth), F32),
            pltpu.SemaphoreType.DMA((columns + 2,)),
        ],
        compiler_params=params(24),
        cost_estimate=pl.CostEstimate(flops=30_000_000, bytes_accessed=4_000_000, transcendentals=0),
        name="inner_updates",
    )(starts, diffusivity, reaction)


def rows_for(array, low_side, reach):
    start = jnp.where(low_side, 0, array.shape[1] - reach)
    return lax.dynamic_slice_in_dim(array, start, reach, axis=1)


def even_pairs():
    return [(i, i ^ 1) for i in range(lax.axis_size("space"))]


def swap_odd(block):
    places = lax.axis_size("space")
    slices = lax.axis_size("tm")

    def partner(time, place):
        if 0 < place < places - 1 or slices % 2:
            return time, (place - 1 if place % 2 == 0 else place + 1) % places
        return time ^ 1, place

    pairs = []
    for time in range(slices):
        for place in range(places):
            other, near = partner(time, place)
            pairs.append((time * places + place, other * places + near))
    return lax.ppermute(block, ("tm", "space"), pairs)


def alive():
    place = lax.axis_index("space")
    last = lax.axis_size("space") - 1
    return jnp.where(jnp.logical_or(place == 0, place == last), 0.0, 1.0).astype(F32)


def mend(low, live, outer, low_ref, high_ref, got_ref, rows_ref, buffers, edges):
    outer_ref, outer_a, outer_b, outer_k = outer
    zero, one, two, three, coef_a, coef_b, coef_k = buffers
    breadth = got_ref.shape[2]
    states = (zero, one, two, three, rows_ref)

    def index(distance):
        return jnp.where(low, 4 + distance, 7 - distance)

    for i in range(4):
        coef_a[4 + i] = outer_a[1 + i]
        coef_b[4 + i] = outer_b[1 + i]
        coef_k[4 + i] = outer_k[1 + i]
    set_coefs(got_ref[4], got_ref[5], coef_a, coef_b, coef_k, index(-1))
    zero[index(-1)] = got_ref[0] * live
    one[index(-2)] = got_ref[2] * live
    at = jnp.where(low, 4, 6)
    for i in range(2):
        zero[at + i] = outer_ref[jnp.where(low, 1, 3) + i]

    @pl.when(low)
    def _():
        for step in range(1, 4):
            for i in range(2):
                states[step][4 + step + i] = low_ref[2 * step - 2 + i]

    @pl.when(jnp.logical_not(low))
    def _():
        for step in range(1, 4):
            for i in range(2):
                states[step][6 - step + i] = high_ref[2 * step - 2 + i]

    toward = jnp.where(low, -0.5 * VEL * DT, 0.5 * VEL * DT)
    one[index(-1)] = (got_ref[1] + (DT * got_ref[4] + toward) * zero[index(0)]) * live
    two[index(-2)] = (got_ref[3] + (DT * got_ref[6] + toward) * one[index(-1)]) * live
    for step in range(1, 5):
        for distance in range(0 if step in (1, 4) else -1, step):
            at = index(distance)
            tiles = fine_row(states[step - 1], at, coef_a, coef_b, coef_k, at, breadth, edges)
            if distance < 0:
                tiles = [t * live for t in tiles]
            put_tiles(states[step], at - 4 if step == 4 else at, tiles)


def even_edge_kernel(
    u_ref, k_ref, g_ref, low_ref, high_ref, got_ref, end_in, rows_ref, end_ref, odd_own, odd_a, odd_b, odd_k,
    k_wide, g_wide, even_own, even_a, even_b, even_k, *buffers
):
    breadth = got_ref.shape[2]
    small = end_ref.shape[0]
    low = parity() == 1

    def fill(high):
        for side, own, coefs in ((high, even_own, (even_a, even_b, even_k)), (1 - high, odd_own, (odd_a, odd_b, odd_k))):
            u_rows, k_rows, g_rows = side_rows(side, u_ref, k_ref, g_ref, k_wide, g_wide)
            for i in range(4):
                own[1 + i] = u_rows[(4 if side else 0) + i]
                set_coefs(k_rows[i], g_rows[i], *coefs, 1 + i)

    @pl.when(low)
    def _():
        fill(0)

    @pl.when(jnp.logical_not(low))
    def _():
        fill(1)

    outer = (even_own, even_a, even_b, even_k)
    mend(low, 1.0, outer, low_ref, high_ref, got_ref, rows_ref, buffers, masks())
    end_ref[...] = end_in[...]
    pool = pool_matrix(breadth, 1.0 / 16.0)
    end_ref[jnp.where(low, 0, small - 1)] = pooled(rows_ref, 0, 1, pool)


def even_edge(starts, diffusivity, reaction, low, high, got, end):
    breadth = got.shape[2]
    side = struct(5, 8, breadth)
    outs = pl.pallas_call(
        even_edge_kernel,
        out_shape=[struct(4, 8, breadth), struct(*end.shape), side, side, side, side],
        in_specs=[VMEM] * 7,
        out_specs=[VMEM] * 6,
        scratch_shapes=[pltpu.VMEM((8, 16, breadth), F32)] * 2
        + [pltpu.VMEM((5, 8, breadth), F32)] * 4
        + [pltpu.VMEM((12, 8, breadth), F32)] * 7,
        compiler_params=params(16),
        name="even_edge",
    )(starts, diffusivity, reaction, low, high, got, end)
    return outs[0], outs[1], outs[2:]


def edge_kernel(
    outer_ref, outer_a, outer_b, outer_k, low_ref, high_ref, got_ref, even_ref, end_in, coarse_ref,
    rows_ref, end_ref, jump_ref, zero, one, two, three, coef_a, coef_b, coef_k, seen, half, coarse_k, coarse_g,
):
    breadth = got_ref.shape[2]
    small = end_ref.shape[0]
    low_side = parity() == 0
    live = alive()
    edges = masks()
    outer = (outer_ref, outer_a, outer_b, outer_k)
    buffers = (zero, one, two, three, coef_a, coef_b, coef_k)
    mend(low_side, live, outer, low_ref, high_ref, got_ref, rows_ref, buffers, edges)
    pool = pool_matrix(breadth, 1.0 / 16.0)
    end_ref[...] = end_in[...]
    end_ref[jnp.where(low_side, 0, small - 1)] = pooled(rows_ref, 0, 1, pool)

    thin = breadth // 4
    odd_at = jnp.where(low_side, 0, 2 + small)
    even_at = jnp.where(low_side, 2 + small, 0)
    near = jnp.where(low_side, 1, 2 + small)
    far = jnp.where(low_side, 2 + small, 1)
    for r in range(small):
        seen[2 + r] = coarse_ref[0, r]
        coarse_k[2 + r] = coarse_ref[1, r]
        coarse_g[2 + r] = coarse_ref[2, r]
    for i in range(2):
        span = slice(i * thin, (i + 1) * thin)
        seen[odd_at + i] = got_ref[7, :, span] * live
        seen[even_at + i] = even_ref[0, :, span]
    for i, ref in ((2, coarse_k), (3, coarse_g)):
        span = slice(i * thin, (i + 1) * thin)
        ref[near] = got_ref[7, :, span]
        ref[far] = even_ref[0, :, span]
    coarse_sweep(seen, half, coarse_k, coarse_g, 1, small + 3, 2, small, low_side, live, edges)
    first = lax.axis_index("tm") == 0
    for r in range(small):
        tiles = coarse_row(half, 2 + r, coarse_k, coarse_g, 2 + r, thin, edges)
        for i, tile in enumerate(tiles):
            span = slice(i * LANES, (i + 1) * LANES)
            jump_ref[r, :, span] = end_ref[r, :, span] - jnp.where(first, 0.0, tile)


def fill_coarse(wide, own, even_part, odd_part, reach, low_side, live):
    rows = own.shape[0]
    count = even_part.shape[0]
    for r in range(rows):
        wide[reach + r] = own[r]
    odd_at = jnp.where(low_side, 0, reach + rows)
    even_at = jnp.where(low_side, reach + rows, 0)
    odd_from = jnp.where(low_side, count - reach, 0)
    even_from = jnp.where(low_side, 0, count - reach)
    for i in range(reach):
        wide[odd_at + i] = odd_part[odd_from + i] * live
        wide[even_at + i] = even_part[even_from + i]


def coarse_sweep(source, target, coef_k, coef_g, low, high, reach, rows, low_side, live, edges, shift=0):
    breadth = source.shape[2]
    for row in range(low, high):
        tiles = coarse_row(source, row, coef_k, coef_g, row + shift, breadth, edges)
        if row < reach:
            factor = jnp.where(low_side, live, 1.0)
            tiles = [t * factor for t in tiles]
        elif row >= reach + rows:
            factor = jnp.where(low_side, 1.0, live)
            tiles = [t * factor for t in tiles]
        put_tiles(target, row, tiles)


def edge(outer, low, high, got, even_got, end, coarse):
    breadth = got.shape[2]
    small = end.shape[0]
    wide = pltpu.VMEM((12, 8, breadth), F32)
    thin = pltpu.VMEM((small + 4, 8, breadth // 4), F32)
    return pl.pallas_call(
        edge_kernel,
        out_shape=[
            struct(4, 8, breadth),
            struct(small, 8, breadth // 4),
            struct(small, 8, breadth // 4),
        ],
        in_specs=[VMEM] * 10,
        out_specs=[VMEM] * 3,
        scratch_shapes=[wide] * 7 + [thin] * 4,
        compiler_params=params(16),
        name="edge_updates",
    )(*outer, low, high, got, even_got, end, coarse)


def last_kernel(behind, *refs):
    before, refs = refs[:behind], refs[behind:]
    fine_hbm, odd_rows, even_rows, end_ref, jump_ref, even_j, odd_j, coarse_ref, even_c, odd_c, out_hbm = refs[:11]
    fine_ref, out_ref, one, two, coarse_k, coarse_g, added, change, moved, sems = refs[11:]
    reach = COARSE * behind
    height, breadth = out_hbm.shape[2:]
    columns = breadth // LANES
    small = height // 4
    fetch = pltpu.make_async_copy(fine_hbm, fine_ref, sems.at[8])
    fetch.start()
    low_side = parity() == 0
    live = alive()
    edges = masks()
    slice_id = lax.axis_index("tm")
    fill_coarse(coarse_k, coarse_ref.at[1], even_c.at[0], odd_c.at[0], reach, low_side, live)
    fill_coarse(coarse_g, coarse_ref.at[2], even_c.at[1], odd_c.at[1], reach, low_side, live)
    at = 0
    for j in range(behind):
        width = reach - COARSE * j
        ok = jnp.where(slice_id >= behind - j, 1.0, 0.0).astype(F32)
        target = one if j == 0 else added
        base = reach - width
        for r in range(small):
            target[reach + r] = before[j][r] * ok
        odd_at = jnp.where(low_side, base, reach + small)
        even_at = jnp.where(low_side, reach + small, base)
        for i in range(width):
            target[odd_at + i] = odd_j[at + i] * (ok * live)
            target[even_at + i] = even_j[at + i] * ok
        at += width
        if j > 0:
            for r in range(base, reach + small + width):
                one[r] = one[r] + added[r]
        coarse_sweep(one, two, coarse_k, coarse_g, base + 1, reach + small + width - 1, reach, small, low_side, live, edges)
        coarse_sweep(two, one, coarse_k, coarse_g, base + 2, reach + small + width - 2, reach, small, low_side, live, edges)
    for r in range(small):
        change[:, r, :] = (one[reach + r] + jump_ref[r]) - end_ref[r]
    spread = spread_matrix(breadth)
    moved[...] = split_dot(change[...].reshape(8 * small, breadth // 4), spread).reshape(8, small, breadth)
    fetch.wait()

    def fix(low_ref, high_ref):
        for x in range(columns):
            for i in range(4):
                fine_ref[:, x, i, :] = low_ref[i, :, x * LANES : (x + 1) * LANES]
                fine_ref[:, x, height - 4 + i, :] = high_ref[i, :, x * LANES : (x + 1) * LANES]

    @pl.when(low_side)
    def _():
        fix(odd_rows, even_rows)

    @pl.when(jnp.logical_not(low_side))
    def _():
        fix(even_rows, odd_rows)

    lower = lax.broadcasted_iota(jnp.int32, (8, LANES), 0) < 4

    def body(z, carry):
        for x in range(columns):
            span = slice(x * LANES, (x + 1) * LANES)
            for row in range(0, height, 8):
                c = row // 4
                step = jnp.where(lower, moved[z, c : c + 1, span], moved[z, c + 1 : c + 2, span])
                out_ref[z, row : row + 8, span] = fine_ref[z, x, row : row + 8, :] + step
        pltpu.make_async_copy(out_ref.at[z], out_hbm.at[0, z], sems.at[z]).start()
        return carry

    lax.fori_loop(0, 8, body, 0)
    for z in range(8):
        pltpu.make_async_copy(out_ref.at[z], out_hbm.at[0, z], sems.at[z]).wait()


def last(fine, rows, even_rows, end, jump, before, even_j, odd_j, coarse, even_c, odd_c, height):
    breadth = rows.shape[2]
    small = height // 4
    reach = COARSE * len(before)
    thin = pltpu.VMEM((small + 2 * reach, 8, breadth // 4), F32)
    return pl.pallas_call(
        functools.partial(last_kernel, len(before)),
        out_shape=struct(1, 8, height, breadth),
        in_specs=[VMEM] * len(before) + [ANY] + [VMEM] * 9,
        out_specs=HBM,
        scratch_shapes=[pltpu.VMEM(fine.shape, F32), pltpu.VMEM((8, height, breadth), F32)]
        + [thin] * 5
        + [
            pltpu.VMEM((8, small, breadth // 4), F32),
            pltpu.VMEM((8, small, breadth), F32),
            pltpu.SemaphoreType.DMA((9,)),
        ],
        compiler_params=params(16),
        name="chain_and_spread",
    )(*before, fine, rows, even_rows, end, jump, even_j, odd_j, coarse, even_c, odd_c)


def relay(jump, coarse, even_c, odd_c, even):
    low_side = parity() == 0
    live = alive()
    small = jump.shape[0]

    def widened(own, even_part, odd_part):
        odd_part = odd_part * live
        low = jnp.where(low_side, odd_part, even_part)
        high = jnp.where(low_side, even_part, odd_part)
        return jnp.concatenate([low, own, high], axis=1)

    def update(values, k, g):
        rows = values.shape[0] - 2
        middle = values[1:-1]
        plus = values[2:] + jnp.pad(middle, ((0, 0), (0, 0), (0, 1)))[:, :, 1:]
        minus = values[:-2] + jnp.pad(middle, ((0, 0), (0, 0), (1, 0)))[:, :, :-1]
        levels = jnp.pad(middle, ((0, 0), (0, 1), (0, 0)))[:, 1:] + jnp.pad(middle, ((0, 0), (1, 0), (0, 0)))[:, :-1]
        bend = levels - 2.0 * middle + (plus + minus - 4.0 * middle) / 16.0
        drift = VEL * (plus - minus) / 8.0
        return middle + (k * bend - 2.0 * DT * drift + g * (middle - middle * middle * middle / 3.0))

    coefs = widened(coarse[1:], even_c, odd_c)
    place = lax.axis_index("space")
    start = jnp.where(place == 0, 1, 0)
    stop = jnp.where(place == lax.axis_size("space") - 1, small + 1, small + 2)
    row = jnp.arange(small + 2)[:, None, None]
    inside = jnp.logical_and(row >= start, row < stop)

    def advance(values):
        block = values[None]
        even_v = lax.ppermute(rows_for(block, jnp.logical_not(low_side), 2), "space", even)
        odd_v = swap_odd(rows_for(block, low_side, 2))
        wide = widened(block, even_v, odd_v)[0]
        wide = jnp.where(inside, update(wide, coefs[0, 1:-1], coefs[1, 1:-1]), 0.0)
        return update(wide, coarse[1], coarse[2])

    slice_id = lax.axis_index("tm")
    slices = lax.axis_size("tm")
    onward = [(i, i + 1) for i in range(slices - 1)]

    def link(position, state):
        incoming = lax.ppermute(state, "tm", onward)
        return jnp.where(slice_id > 0, advance(incoming), 0.0) + jump

    return lax.fori_loop(0, slices - 1, link, jump)


def per_device(starts, diffusivity, reaction):
    height, breadth = starts.shape[2:]
    small = height // 4
    slices = lax.axis_size("tm")
    behind = slices - 1
    reach = COARSE * behind
    at_once = 0 < behind and reach <= small
    even = even_pairs()
    low_side = parity() == 0
    high_side = jnp.logical_not(low_side)

    odd_rows = odd_pack(starts, diffusivity, reaction)
    odd_got = swap_odd(odd_rows)
    even_rows, even_rest = even_pack(odd_rows, starts, diffusivity, reaction)
    even_got = lax.ppermute(even_rows, "space", even)
    even_got_rest = lax.ppermute(even_rest, "space", even)
    fine, low_steps, high_steps, coarse, end = inner(starts, diffusivity, reaction)
    mended, end, odd_outer = even_edge(starts, diffusivity, reaction, low_steps, high_steps, even_got, end)
    rows, end, jump = edge(odd_outer, low_steps, high_steps, odd_got, even_got_rest, end, coarse)
    width = reach if at_once else COARSE
    later, jump = lax.optimization_barrier((coarse[1:], jump))
    odd_c = swap_odd(rows_for(later, low_side, width))
    even_c = lax.ppermute(rows_for(later, high_side, width), "space", even)
    if at_once:
        before = [
            lax.ppermute(jump, "tm", [(i, (i + k) % slices) for i in range(slices)])
            for k in range(behind, 0, -1)
        ]

        def halo(low):
            return jnp.concatenate(
                [rows_for(before[j][None], low, reach - COARSE * j)[0] for j in range(behind)], axis=0
            )

        odd_j = swap_odd(halo(low_side))
        even_j = lax.ppermute(halo(high_side), "space", even)
        return last(fine, rows, mended, end, jump, before, even_j, odd_j, coarse, even_c, odd_c, height)
    chained = relay(jump, coarse, even_c, odd_c, even)
    change = jnp.repeat(jnp.repeat(jnp.transpose(chained - end, (1, 0, 2)), 4, axis=1), 4, axis=2)
    fixed = jnp.where(low_side, 0, height - 4)
    fine = jnp.transpose(fine, (0, 2, 1, 3)).reshape(8, height, breadth)
    fine = lax.dynamic_update_slice_in_dim(fine, jnp.transpose(rows, (1, 0, 2)), fixed, axis=1)
    fine = lax.dynamic_update_slice_in_dim(fine, jnp.transpose(mended, (1, 0, 2)), height - 4 - fixed, axis=1)
    return (fine + change)[None]


def solution(mesh):
    in_specs = (P("tm", None, "space", None), P(None, "space", None), P(None, "space", None))
    out_specs = P("tm", None, "space", None)
    return jax.shard_map(per_device, mesh=mesh, in_specs=in_specs, out_specs=out_specs, check_vma=False)
```

```python
import functools

import jax
import jax.numpy as jnp
from jax import lax
from jax.experimental import pallas as pl
from jax.experimental.pallas import tpu as pltpu
from jax.sharding import PartitionSpec as P

FINE = 4
COARSE = 2
DT = 0.05
VEL = 0.5
LANES = 128
F32 = jnp.float32
BF16 = jnp.bfloat16
ODD_MIB = 53.4

VMEM = pl.BlockSpec(memory_space=pltpu.VMEM)
ANY = pl.BlockSpec(memory_space=pl.ANY)
HBM = pl.BlockSpec(memory_space=pltpu.HBM)


def params(mib):
    return pltpu.CompilerParams(vmem_limit_bytes=int(mib * 2**20))


def struct(*shape):
    return jax.ShapeDtypeStruct(shape, F32)


def parity():
    return lax.rem(lax.axis_index("space"), 2)


def tiles_of(ref, row, breadth):
    return [ref[row, :, i : i + LANES] for i in range(0, breadth, LANES)]


def put_tiles(ref, row, tiles):
    for i, tile in enumerate(tiles):
        ref[row, :, i * LANES : (i + 1) * LANES] = tile


def masks():
    lane = lax.broadcasted_iota(jnp.int32, (8, LANES), 1)
    level = lax.broadcasted_iota(jnp.int32, (8, LANES), 0)
    return lane == 0, lane == LANES - 1, level == 0, level == 7


def neighbours(tiles, edges):
    first, last, bottom, top = edges
    back = [pltpu.roll(t, LANES - 1, 1) for t in tiles]
    forth = [pltpu.roll(t, 1, 1) for t in tiles]
    zero = jnp.zeros_like(tiles[0])
    x_next = [jnp.where(last, b, a) for a, b in zip(back, back[1:] + [zero])]
    x_prev = [jnp.where(first, b, a) for a, b in zip(forth, [zero] + forth[:-1])]
    levels = [
        jnp.where(top, 0.0, pltpu.roll(t, 7, 0)) + jnp.where(bottom, 0.0, pltpu.roll(t, 1, 0))
        for t in tiles
    ]
    return x_next, x_prev, levels


def fine_row(state, row, coef_a, coef_b, coef_k, coef_row, breadth, edges):
    tiles = tiles_of(state, row, breadth)
    x_next, x_prev, levels = neighbours(tiles, edges)
    out = []
    for i, u in enumerate(tiles):
        span = slice(i * LANES, (i + 1) * LANES)
        plus = state[row + 1, :, span] + x_next[i]
        minus = state[row - 1, :, span] + x_prev[i]
        own = u * (coef_a[coef_row, :, span] - coef_b[coef_row, :, span] * (u * u))
        spread = coef_k[coef_row, :, span] * ((plus + minus) + levels[i])
        out.append((own + spread) - (0.5 * VEL * DT) * (plus - minus))
    return out


def coarse_row(state, row, coef_k, coef_g, coef_row, breadth, edges):
    tiles = tiles_of(state, row, breadth)
    x_next, x_prev, levels = neighbours(tiles, edges)
    out = []
    for i, c in enumerate(tiles):
        span = slice(i * LANES, (i + 1) * LANES)
        plus = state[row + 1, :, span] + x_next[i]
        minus = state[row - 1, :, span] + x_prev[i]
        k = coef_k[coef_row, :, span]
        g = coef_g[coef_row, :, span]
        bend = (levels[i] - 2.0 * c) + ((plus + minus) - 4.0 * c) * (1.0 / 16.0)
        drift = (2.0 * DT * VEL / 8.0) * (plus - minus)
        out.append(c + ((k * bend - drift) + g * (c - c * c * c * (1.0 / 3.0))))
    return out


def split_dot(values, matrix):
    high = values.astype(BF16)
    low = (values - high.astype(F32)).astype(BF16)
    both = jnp.dot(jnp.concatenate([high, low], axis=0), matrix, preferred_element_type=F32)
    rows = values.shape[0]
    return both[:rows] + both[rows:]


def pool_matrix(breadth, value):
    fine = lax.broadcasted_iota(jnp.int32, (breadth, breadth // 4), 0)
    coarse = lax.broadcasted_iota(jnp.int32, (breadth, breadth // 4), 1)
    return jnp.where(fine // 4 == coarse, value, 0.0).astype(BF16)


def spread_matrix(breadth):
    coarse = lax.broadcasted_iota(jnp.int32, (breadth // 4, breadth), 0)
    fine = lax.broadcasted_iota(jnp.int32, (breadth // 4, breadth), 1)
    return jnp.where(fine // 4 == coarse, 1.0, 0.0).astype(BF16)


def pooled(ref, first_row, coarse_rows, pool):
    sums = []
    for c in range(coarse_rows):
        r = first_row + 4 * c
        sums.append((ref[r] + ref[r + 1]) + (ref[r + 2] + ref[r + 3]))
    return split_dot(jnp.concatenate(sums, axis=0), pool)


def set_coefs(k, g, a_ref, b_ref, k_ref, row):
    k = DT * k
    g = DT * g
    k_ref[row] = k
    b_ref[row] = g * (1.0 / 3.0)
    a_ref[row] = 1.0 + (g - 6.0 * k)


def put_pooled(ref, row, sums, pool):
    thin = ref.shape[2] // 4
    small = split_dot(jnp.concatenate(sums, axis=0), pool)
    for i in range(4):
        value = small[8 * i : 8 * i + 8] * (1.0 if i < 2 else 2.0 * DT)
        ref[row, :, i * thin : (i + 1) * thin] = value


def sums_of_four(*arrays):
    return [(r[0] + r[1]) + (r[2] + r[3]) for r in arrays]


def message(high, u_rows, k_rows, g_rows, ref, last_ref, last_row, state, after, coefs, pool, edges):
    breadth = ref.shape[2]
    near = 4 if high else 1
    step = -1 if high else 1
    zeros = jnp.zeros((8, breadth), F32)
    state[0] = zeros
    state[5] = zeros
    after[0] = zeros
    after[3] = zeros
    for i in range(4):
        state[1 + i] = u_rows[(4 if high else 0) + i]
        set_coefs(k_rows[i], g_rows[i], *coefs, 1 + i)
    ref[0] = state[near]
    put_tiles(ref, 1, fine_row(state, near, *coefs, near, breadth, edges))
    one = fine_row(state, near + step, *coefs, near + step, breadth, edges)
    two = fine_row(state, near + 2 * step, *coefs, near + 2 * step, breadth, edges)
    put_tiles(ref, 2, one)
    place = 2 if high else 1
    put_tiles(after, place, one)
    put_tiles(after, place + step, two)
    put_tiles(ref, 3, fine_row(after, place, *coefs, near + step, breadth, edges))
    ref[4] = k_rows[near - 1]
    ref[5] = g_rows[near - 1]
    ref[6] = k_rows[near - 1 + step]
    put_pooled(last_ref, last_row, sums_of_four(u_rows[:4], u_rows[4:], k_rows, g_rows), pool)


def odd_kernel(
    u_hbm, k_hbm, g_hbm, odd_ref, u_nat, k_nat, g_nat, k_wide, g_wide, state, after, coef_a, coef_b, coef_k, sems
):
    height, breadth = u_hbm.shape[2:]
    low_side = parity() == 0
    row8 = pl.multiple_of(jnp.where(low_side, 0, height - 8), 8)
    row16 = pl.multiple_of(jnp.where(low_side, 0, height - 16), 16)
    copies = [
        pltpu.make_async_copy(u_hbm.at[0, :, pl.ds(row8, 8), :], u_nat, sems.at[0]),
        pltpu.make_async_copy(k_hbm.at[:, pl.ds(row16, 16), :], k_nat, sems.at[1]),
        pltpu.make_async_copy(g_hbm.at[:, pl.ds(row16, 16), :], g_nat, sems.at[2]),
    ]
    for copy in copies:
        copy.start()
    pool = pool_matrix(breadth, 1.0 / 16.0)
    edges = masks()
    for copy in copies:
        copy.wait()
    k_wide[...] = k_nat[...].astype(F32)
    g_wide[...] = g_nat[...].astype(F32)

    def fill(high):
        low = 12 if high else 0
        u_rows = [u_nat[:, i, :] for i in range(8)]
        k_rows = [k_wide[:, low + i, :] for i in range(4)]
        g_rows = [g_wide[:, low + i, :] for i in range(4)]
        coefs = (coef_a, coef_b, coef_k)
        message(high, u_rows, k_rows, g_rows, odd_ref, odd_ref, 7, state, after, coefs, pool, edges)

    @pl.when(low_side)
    def _():
        fill(0)

    @pl.when(jnp.logical_not(low_side))
    def _():
        fill(1)


def odd_pack(starts, diffusivity, reaction):
    breadth = starts.shape[3]
    coef = pltpu.VMEM((6, 8, breadth), F32)
    return pl.pallas_call(
        odd_kernel,
        out_shape=struct(8, 8, breadth),
        in_specs=[HBM] * 3,
        out_specs=VMEM,
        scratch_shapes=[
            pltpu.VMEM((8, 8, breadth), F32),
            pltpu.VMEM((8, 16, breadth), BF16),
            pltpu.VMEM((8, 16, breadth), BF16),
            pltpu.VMEM((8, 16, breadth), F32),
            pltpu.VMEM((8, 16, breadth), F32),
            coef,
            pltpu.VMEM((4, 8, breadth), F32),
            coef,
            coef,
            coef,
            pltpu.SemaphoreType.DMA((3,)),
        ],
        compiler_params=params(ODD_MIB),
        name="odd_rows",
    )(starts, diffusivity, reaction)


def side_rows(high, u_ref, k_ref, g_ref, k_wide, g_wide):
    height = u_ref.shape[2]
    k_wide[...] = k_ref[:, height - 16 if high else 0 : height if high else 16, :].astype(F32)
    g_wide[...] = g_ref[:, height - 16 if high else 0 : height if high else 16, :].astype(F32)
    low = 12 if high else 0
    u_rows = [u_ref[0, :, (height - 8 if high else 0) + i, :] for i in range(8)]
    k_rows = [k_wide[:, low + i, :] for i in range(4)]
    g_rows = [g_wide[:, low + i, :] for i in range(4)]
    return u_rows, k_rows, g_rows


def even_kernel(odd_rows, u_ref, k_ref, g_ref, even_ref, rest_ref, k_wide, g_wide, state, after, coef_a, coef_b, coef_k):
    del odd_rows
    pool = pool_matrix(u_ref.shape[3], 1.0 / 16.0)
    edges = masks()

    def fill(high):
        coefs = (coef_a, coef_b, coef_k)
        rows = side_rows(high, u_ref, k_ref, g_ref, k_wide, g_wide)
        message(high, *rows, even_ref, rest_ref, 0, state, after, coefs, pool, edges)

    above = parity() == 0

    @pl.when(above)
    def _():
        fill(1)

    @pl.when(jnp.logical_not(above))
    def _():
        fill(0)


def even_pack(odd_rows, starts, diffusivity, reaction):
    breadth = starts.shape[3]
    coef = pltpu.VMEM((6, 8, breadth), F32)
    return pl.pallas_call(
        even_kernel,
        out_shape=[struct(7, 8, breadth), struct(1, 8, breadth)],
        in_specs=[ANY] + [VMEM] * 3,
        out_specs=[VMEM] * 2,
        scratch_shapes=[pltpu.VMEM((8, 16, breadth), F32)] * 2
        + [coef, pltpu.VMEM((4, 8, breadth), F32), coef, coef, coef],
        compiler_params=params(16),
        name="even_rows",
    )(odd_rows, starts, diffusivity, reaction)


def pooled_into(flat, targets, scales, pool):
    count = len(targets)
    _, _, small, breadth = flat.shape
    thin = breadth // 4
    means = split_dot(flat[0:count].reshape(count * 8 * small, breadth), pool).reshape(count, 8, small, thin)
    for part in range(count):
        flat[part, :, :, 0:thin] = means[part] * scales[part]
        for r in range(small):
            targets[part][r] = flat[part, :, r, 0:thin]


def sums_of(ref, level, start, flat, part):
    small = flat.shape[2]

    def body(z, carry):
        for x in range(ref.shape[1]):
            rows = [ref[z + level, x, pl.ds(start + i, small, stride=4), :] for i in range(4)]
            flat[part, z, :, x * LANES : (x + 1) * LANES] = (rows[0] + rows[1]) + (rows[2] + rows[3])
        return carry

    lax.fori_loop(0, 8, body, 0, unroll=2)


def clear_ends(ref, top):
    blank = jnp.zeros((8, LANES), F32)
    columns = ref.shape[1]

    def clear(z, carry):
        for x in range(columns):
            ref[z, x, 0:8, :] = blank
            ref[z, x, top : top + 8, :] = blank
        return carry

    lax.fori_loop(0, 10, clear, 0)
    for z in (0, 9):
        for x in range(columns):
            ref[z, x, 8:top, :] = jnp.zeros((top - 8, LANES), F32)


def inner_kernel(
    u_hbm, k_hbm, g_hbm, fine_ref, low_ref, high_ref, coarse_ref, end_ref,
    one, two, coef_a, coef_b, coef_k, k_nat, g_nat, flat, sems,
):
    height, breadth = u_hbm.shape[2:]
    columns = breadth // LANES
    spans = [slice(x * LANES, (x + 1) * LANES) for x in range(columns)]
    top = height + 8
    copies = [
        pltpu.make_async_copy(
            u_hbm.at[0, :, :, pl.ds(x * LANES, LANES)], one.at[pl.ds(1, 8), x, pl.ds(8, height), :], sems.at[x]
        )
        for x in range(columns)
    ]
    k_copy = pltpu.make_async_copy(k_hbm, k_nat, sems.at[columns])
    g_copy = pltpu.make_async_copy(g_hbm, g_nat, sems.at[columns + 1])
    for copy in [k_copy, g_copy] + copies:
        copy.start()
    clear_ends(one, top)
    clear_ends(two, top)
    pool = pool_matrix(breadth, 1.0 / 16.0)
    k_copy.wait()
    g_copy.wait()

    def widen(z, carry):
        for x, span in enumerate(spans):
            for r in range(0, height, 16):
                k = DT * k_nat[z, r : r + 16, span].astype(F32)
                g = DT * g_nat[z, r : r + 16, span].astype(F32)
                coef_k[z, x, r : r + 16, :] = k
                coef_b[z, x, r : r + 16, :] = g * (1.0 / 3.0)
                coef_a[z, x, r : r + 16, :] = 1.0 + (g - 6.0 * k)
        return carry

    lax.fori_loop(0, 8, widen, 0)
    for copy in copies:
        copy.wait()
    sums_of(one, 1, 8, flat, 0)
    sums_of(coef_k, 0, 0, flat, 1)
    sums_of(coef_b, 0, 0, flat, 2)
    pooled_into(flat, [coarse_ref.at[0], coarse_ref.at[1], coarse_ref.at[2]], (1.0, 2.0, 6.0), pool)

    lane = lax.broadcasted_iota(jnp.int32, (8, LANES), 1)
    first, final = lane == 0, lane == LANES - 1
    blank = jnp.zeros((8, LANES), F32)

    def sweep(source, target, level, shift):
        def body(z, carry):
            for row in range(8, top, 8):
                tiles = [source[z + 1, x, row : row + 8, :] for x in range(columns)]
                back = [pltpu.roll(t, LANES - 1, 1) for t in tiles] + [blank]
                forth = [blank] + [pltpu.roll(t, 1, 1) for t in tiles]
                for x, u in enumerate(tiles):
                    x_next = jnp.where(final, back[x + 1], back[x])
                    x_prev = jnp.where(first, forth[x], forth[x + 1])
                    plus = source[z + 1, x, row + 1 : row + 9, :] + x_next
                    minus = source[z + 1, x, row - 1 : row + 7, :] + x_prev
                    levels = source[z, x, row : row + 8, :] + source[z + 2, x, row : row + 8, :]
                    rows = slice(row - 8, row)
                    own_part = u * (coef_a[z, x, rows, :] - coef_b[z, x, rows, :] * (u * u))
                    spread = coef_k[z, x, rows, :] * ((plus + minus) + levels)
                    out = (own_part + spread) - (0.5 * VEL * DT) * (plus - minus)
                    target[z + level, x, row + shift : row + shift + 8, :] = out
            return carry

        lax.fori_loop(0, 8, body, 0, unroll=8)

    def keep(step, source):
        for x, span in enumerate(spans):
            for i in range(2):
                low_ref[2 * step - 2 + i, :, span] = source[1:9, x, 8 + step + i, :]
                high_ref[2 * step - 2 + i, :, span] = source[1:9, x, top - 2 - step + i, :]

    sweep(one, two, 1, 0)
    keep(1, two)
    sweep(two, one, 1, 0)
    keep(2, one)
    sweep(one, two, 1, 0)
    keep(3, two)
    sweep(two, fine_ref, 0, -8)
    sums_of(fine_ref, 0, 0, flat, 0)
    pooled_into(flat, [end_ref], (1.0,), pool)


def inner(starts, diffusivity, reaction):
    height, breadth = starts.shape[2:]
    small = height // 4
    columns = breadth // LANES
    wide = pltpu.VMEM((10, columns, height + 16, LANES), F32)
    coef = pltpu.VMEM((8, columns, height, LANES), F32)
    return pl.pallas_call(
        inner_kernel,
        out_shape=[
            struct(8, columns, height, LANES),
            struct(6, 8, breadth),
            struct(6, 8, breadth),
            struct(3, small, 8, breadth // 4),
            struct(small, 8, breadth // 4),
        ],
        in_specs=[ANY] * 3,
        out_specs=[VMEM] * 5,
        scratch_shapes=[wide, wide, coef, coef, coef]
        + [
            pltpu.VMEM((8, height, breadth), BF16),
            pltpu.VMEM((8, height, breadth), BF16),
            pltpu.VMEM((3, 8, small, breadth), F32),
            pltpu.SemaphoreType.DMA((columns + 2,)),
        ],
        compiler_params=params(24),
        cost_estimate=pl.CostEstimate(flops=30_000_000, bytes_accessed=4_000_000, transcendentals=0),
        name="inner_updates",
    )(starts, diffusivity, reaction)


def rows_for(array, low_side, reach):
    start = jnp.where(low_side, 0, array.shape[1] - reach)
    return lax.dynamic_slice_in_dim(array, start, reach, axis=1)


def even_pairs():
    return [(i, i ^ 1) for i in range(lax.axis_size("space"))]


def swap_odd(block):
    places = lax.axis_size("space")
    slices = lax.axis_size("tm")

    def partner(time, place):
        if 0 < place < places - 1 or slices % 2:
            return time, (place - 1 if place % 2 == 0 else place + 1) % places
        return time ^ 1, place

    pairs = []
    for time in range(slices):
        for place in range(places):
            other, near = partner(time, place)
            pairs.append((time * places + place, other * places + near))
    return lax.ppermute(block, ("tm", "space"), pairs)


def alive():
    place = lax.axis_index("space")
    last = lax.axis_size("space") - 1
    return jnp.where(jnp.logical_or(place == 0, place == last), 0.0, 1.0).astype(F32)


def mend(low, live, outer, low_ref, high_ref, got_ref, rows_ref, buffers, edges):
    outer_ref, outer_a, outer_b, outer_k = outer
    zero, one, two, three, coef_a, coef_b, coef_k = buffers
    breadth = got_ref.shape[2]
    states = (zero, one, two, three, rows_ref)

    def index(distance):
        return jnp.where(low, 4 + distance, 7 - distance)

    for i in range(4):
        coef_a[4 + i] = outer_a[1 + i]
        coef_b[4 + i] = outer_b[1 + i]
        coef_k[4 + i] = outer_k[1 + i]
    set_coefs(got_ref[4], got_ref[5], coef_a, coef_b, coef_k, index(-1))
    zero[index(-1)] = got_ref[0] * live
    one[index(-2)] = got_ref[2] * live
    at = jnp.where(low, 4, 6)
    for i in range(2):
        zero[at + i] = outer_ref[jnp.where(low, 1, 3) + i]

    @pl.when(low)
    def _():
        for step in range(1, 4):
            for i in range(2):
                states[step][4 + step + i] = low_ref[2 * step - 2 + i]

    @pl.when(jnp.logical_not(low))
    def _():
        for step in range(1, 4):
            for i in range(2):
                states[step][6 - step + i] = high_ref[2 * step - 2 + i]

    toward = jnp.where(low, -0.5 * VEL * DT, 0.5 * VEL * DT)
    one[index(-1)] = (got_ref[1] + (DT * got_ref[4] + toward) * zero[index(0)]) * live
    two[index(-2)] = (got_ref[3] + (DT * got_ref[6] + toward) * one[index(-1)]) * live
    for step in range(1, 5):
        for distance in range(0 if step in (1, 4) else -1, step):
            at = index(distance)
            tiles = fine_row(states[step - 1], at, coef_a, coef_b, coef_k, at, breadth, edges)
            if distance < 0:
                tiles = [t * live for t in tiles]
            put_tiles(states[step], at - 4 if step == 4 else at, tiles)


def even_edge_kernel(
    u_ref, k_ref, g_ref, low_ref, high_ref, got_ref, end_in, rows_ref, end_ref, odd_own, odd_a, odd_b, odd_k,
    k_wide, g_wide, even_own, even_a, even_b, even_k, *buffers
):
    breadth = got_ref.shape[2]
    small = end_ref.shape[0]
    low = parity() == 1

    def fill(high):
        for side, own, coefs in ((high, even_own, (even_a, even_b, even_k)), (1 - high, odd_own, (odd_a, odd_b, odd_k))):
            u_rows, k_rows, g_rows = side_rows(side, u_ref, k_ref, g_ref, k_wide, g_wide)
            for i in range(4):
                own[1 + i] = u_rows[(4 if side else 0) + i]
                set_coefs(k_rows[i], g_rows[i], *coefs, 1 + i)

    @pl.when(low)
    def _():
        fill(0)

    @pl.when(jnp.logical_not(low))
    def _():
        fill(1)

    outer = (even_own, even_a, even_b, even_k)
    mend(low, 1.0, outer, low_ref, high_ref, got_ref, rows_ref, buffers, masks())
    end_ref[...] = end_in[...]
    pool = pool_matrix(breadth, 1.0 / 16.0)
    end_ref[jnp.where(low, 0, small - 1)] = pooled(rows_ref, 0, 1, pool)


def even_edge(starts, diffusivity, reaction, low, high, got, end):
    breadth = got.shape[2]
    side = struct(5, 8, breadth)
    outs = pl.pallas_call(
        even_edge_kernel,
        out_shape=[struct(4, 8, breadth), struct(*end.shape), side, side, side, side],
        in_specs=[VMEM] * 7,
        out_specs=[VMEM] * 6,
        scratch_shapes=[pltpu.VMEM((8, 16, breadth), F32)] * 2
        + [pltpu.VMEM((5, 8, breadth), F32)] * 4
        + [pltpu.VMEM((12, 8, breadth), F32)] * 7,
        compiler_params=params(16),
        name="even_edge",
    )(starts, diffusivity, reaction, low, high, got, end)
    return outs[0], outs[1], outs[2:]


def edge_kernel(
    outer_ref, outer_a, outer_b, outer_k, low_ref, high_ref, got_ref, even_ref, end_in, coarse_ref,
    rows_ref, end_ref, jump_ref, zero, one, two, three, coef_a, coef_b, coef_k, seen, half, coarse_k, coarse_g,
):
    breadth = got_ref.shape[2]
    small = end_ref.shape[0]
    low_side = parity() == 0
    live = alive()
    edges = masks()
    outer = (outer_ref, outer_a, outer_b, outer_k)
    buffers = (zero, one, two, three, coef_a, coef_b, coef_k)
    mend(low_side, live, outer, low_ref, high_ref, got_ref, rows_ref, buffers, edges)
    pool = pool_matrix(breadth, 1.0 / 16.0)
    end_ref[...] = end_in[...]
    end_ref[jnp.where(low_side, 0, small - 1)] = pooled(rows_ref, 0, 1, pool)

    thin = breadth // 4
    odd_at = jnp.where(low_side, 0, 2 + small)
    even_at = jnp.where(low_side, 2 + small, 0)
    near = jnp.where(low_side, 1, 2 + small)
    far = jnp.where(low_side, 2 + small, 1)
    for r in range(small):
        seen[2 + r] = coarse_ref[0, r]
        coarse_k[2 + r] = coarse_ref[1, r]
        coarse_g[2 + r] = coarse_ref[2, r]
    for i in range(2):
        span = slice(i * thin, (i + 1) * thin)
        seen[odd_at + i] = got_ref[7, :, span] * live
        seen[even_at + i] = even_ref[0, :, span]
    for i, ref in ((2, coarse_k), (3, coarse_g)):
        span = slice(i * thin, (i + 1) * thin)
        ref[near] = got_ref[7, :, span]
        ref[far] = even_ref[0, :, span]
    coarse_sweep(seen, half, coarse_k, coarse_g, 1, small + 3, 2, small, low_side, live, edges)
    first = lax.axis_index("tm") == 0
    for r in range(small):
        tiles = coarse_row(half, 2 + r, coarse_k, coarse_g, 2 + r, thin, edges)
        for i, tile in enumerate(tiles):
            span = slice(i * LANES, (i + 1) * LANES)
            jump_ref[r, :, span] = end_ref[r, :, span] - jnp.where(first, 0.0, tile)


def fill_coarse(wide, own, even_part, odd_part, reach, low_side, live):
    rows = own.shape[0]
    count = even_part.shape[0]
    for r in range(rows):
        wide[reach + r] = own[r]
    odd_at = jnp.where(low_side, 0, reach + rows)
    even_at = jnp.where(low_side, reach + rows, 0)
    odd_from = jnp.where(low_side, count - reach, 0)
    even_from = jnp.where(low_side, 0, count - reach)
    for i in range(reach):
        wide[odd_at + i] = odd_part[odd_from + i] * live
        wide[even_at + i] = even_part[even_from + i]


def coarse_sweep(source, target, coef_k, coef_g, low, high, reach, rows, low_side, live, edges, shift=0):
    breadth = source.shape[2]
    for row in range(low, high):
        tiles = coarse_row(source, row, coef_k, coef_g, row + shift, breadth, edges)
        if row < reach:
            factor = jnp.where(low_side, live, 1.0)
            tiles = [t * factor for t in tiles]
        elif row >= reach + rows:
            factor = jnp.where(low_side, 1.0, live)
            tiles = [t * factor for t in tiles]
        put_tiles(target, row, tiles)


def edge(outer, low, high, got, even_got, end, coarse):
    breadth = got.shape[2]
    small = end.shape[0]
    wide = pltpu.VMEM((12, 8, breadth), F32)
    thin = pltpu.VMEM((small + 4, 8, breadth // 4), F32)
    return pl.pallas_call(
        edge_kernel,
        out_shape=[
            struct(4, 8, breadth),
            struct(small, 8, breadth // 4),
            struct(small, 8, breadth // 4),
        ],
        in_specs=[VMEM] * 10,
        out_specs=[VMEM] * 3,
        scratch_shapes=[wide] * 7 + [thin] * 4,
        compiler_params=params(16),
        name="edge_updates",
    )(*outer, low, high, got, even_got, end, coarse)


def ready_kernel(
    odd_rows, even_rows, end_ref, jump_ref, coarse_ref, even_c, odd_c, fine_hbm,
    fine_ref, gap_ref, coarse_k, coarse_g, spread_ref, sem,
):
    columns, height = fine_ref.shape[1:3]
    reach = even_c.shape[1]
    small = end_ref.shape[0]
    fetch = pltpu.make_async_copy(fine_hbm, fine_ref, sem)
    fetch.start()
    low_side = parity() == 0
    live = alive()
    fill_coarse(coarse_k, coarse_ref.at[1], even_c.at[0], odd_c.at[0], reach, low_side, live)
    fill_coarse(coarse_g, coarse_ref.at[2], even_c.at[1], odd_c.at[1], reach, low_side, live)
    for r in range(small):
        gap_ref[r] = jump_ref[r] - end_ref[r]
    spread_ref[...] = spread_matrix(columns * LANES)
    fetch.wait()

    def fix(low_ref, high_ref):
        for x in range(columns):
            for i in range(4):
                fine_ref[:, x, i, :] = low_ref[i, :, x * LANES : (x + 1) * LANES]
                fine_ref[:, x, height - 4 + i, :] = high_ref[i, :, x * LANES : (x + 1) * LANES]

    @pl.when(low_side)
    def _():
        fix(odd_rows, even_rows)

    @pl.when(jnp.logical_not(low_side))
    def _():
        fix(even_rows, odd_rows)


def ready(fine, rows, even_rows, end, jump, coarse, even_c, odd_c):
    breadth = rows.shape[2]
    small = end.shape[0]
    thin = struct(small + 2 * even_c.shape[1], 8, breadth // 4)
    return pl.pallas_call(
        ready_kernel,
        out_shape=[
            struct(*fine.shape),
            struct(*end.shape),
            thin,
            thin,
            jax.ShapeDtypeStruct((breadth // 4, breadth), BF16),
        ],
        in_specs=[VMEM] * 7 + [ANY],
        out_specs=[VMEM] * 5,
        scratch_shapes=[pltpu.SemaphoreType.DMA(())],
        compiler_params=params(16),
        name="ready_arrays",
    )(rows, even_rows, end, jump, coarse, even_c, odd_c, fine)


def last_kernel(behind, *refs):
    before, refs = refs[:behind][::-1], refs[behind:]
    fine_ref, gap_ref, even_j, odd_j, coarse_k, coarse_g, spread_ref, out_hbm = refs[:8]
    out_ref, one, two, added, change, moved, sems = refs[8:]
    reach = COARSE * behind
    height, breadth = out_hbm.shape[2:]
    columns = breadth // LANES
    small = height // 4
    low_side = parity() == 0
    live = alive()
    edges = masks()
    slice_id = lax.axis_index("tm")
    at = 0
    for j in range(behind):
        width = reach - COARSE * j
        ok = jnp.where(slice_id >= behind - j, 1.0, 0.0).astype(F32)
        target = one if j == 0 else added
        base = reach - width
        for r in range(small):
            target[reach + r] = before[j][r] * ok
        odd_at = jnp.where(low_side, base, reach + small)
        even_at = jnp.where(low_side, reach + small, base)
        for i in range(width):
            target[odd_at + i] = odd_j[at + i] * (ok * live)
            target[even_at + i] = even_j[at + i] * ok
        at += width
        if j > 0:
            for r in range(base, reach + small + width):
                one[r] = one[r] + added[r]
        coarse_sweep(one, two, coarse_k, coarse_g, base + 1, reach + small + width - 1, reach, small, low_side, live, edges)
        coarse_sweep(two, one, coarse_k, coarse_g, base + 2, reach + small + width - 2, reach, small, low_side, live, edges)
    for r in range(small):
        change[:, r, :] = one[reach + r] + gap_ref[r]
    moved[...] = split_dot(change[...].reshape(8 * small, breadth // 4), spread_ref[...]).reshape(8, small, breadth)
    lower = lax.broadcasted_iota(jnp.int32, (8, LANES), 0) < 4

    def body(z, carry):
        for x in range(columns):
            span = slice(x * LANES, (x + 1) * LANES)
            for row in range(0, height, 8):
                c = row // 4
                step = jnp.where(lower, moved[z, c : c + 1, span], moved[z, c + 1 : c + 2, span])
                out_ref[z, row : row + 8, span] = fine_ref[z, x, row : row + 8, :] + step
        pltpu.make_async_copy(out_ref.at[z], out_hbm.at[0, z], sems.at[z]).start()
        return carry

    lax.fori_loop(0, 8, body, 0)
    for z in range(8):
        pltpu.make_async_copy(out_ref.at[z], out_hbm.at[0, z], sems.at[z]).wait()


def last(before, even_j, odd_j, fine, gap, coarse_k, coarse_g, spread):
    _, columns, height, _ = fine.shape
    breadth = columns * LANES
    small = height // 4
    thin = pltpu.VMEM(coarse_k.shape, F32)
    return pl.pallas_call(
        functools.partial(last_kernel, len(before)),
        out_shape=struct(1, 8, height, breadth),
        in_specs=[VMEM] * (len(before) + 7),
        out_specs=HBM,
        scratch_shapes=[
            pltpu.VMEM((8, height, breadth), F32),
            thin,
            thin,
            thin,
            pltpu.VMEM((8, small, breadth // 4), F32),
            pltpu.VMEM((8, small, breadth), F32),
            pltpu.SemaphoreType.DMA((8,)),
        ],
        compiler_params=params(16),
        name="chain_and_spread",
    )(*before[::-1], fine, gap, even_j, odd_j, coarse_k, coarse_g, spread)


def relay(jump, coarse, even_c, odd_c, even):
    low_side = parity() == 0
    live = alive()
    small = jump.shape[0]

    def widened(own, even_part, odd_part):
        odd_part = odd_part * live
        low = jnp.where(low_side, odd_part, even_part)
        high = jnp.where(low_side, even_part, odd_part)
        return jnp.concatenate([low, own, high], axis=1)

    def update(values, k, g):
        rows = values.shape[0] - 2
        middle = values[1:-1]
        plus = values[2:] + jnp.pad(middle, ((0, 0), (0, 0), (0, 1)))[:, :, 1:]
        minus = values[:-2] + jnp.pad(middle, ((0, 0), (0, 0), (1, 0)))[:, :, :-1]
        levels = jnp.pad(middle, ((0, 0), (0, 1), (0, 0)))[:, 1:] + jnp.pad(middle, ((0, 0), (1, 0), (0, 0)))[:, :-1]
        bend = levels - 2.0 * middle + (plus + minus - 4.0 * middle) / 16.0
        drift = VEL * (plus - minus) / 8.0
        return middle + (k * bend - 2.0 * DT * drift + g * (middle - middle * middle * middle / 3.0))

    coefs = widened(coarse[1:], even_c, odd_c)
    place = lax.axis_index("space")
    start = jnp.where(place == 0, 1, 0)
    stop = jnp.where(place == lax.axis_size("space") - 1, small + 1, small + 2)
    row = jnp.arange(small + 2)[:, None, None]
    inside = jnp.logical_and(row >= start, row < stop)

    def advance(values):
        block = values[None]
        even_v = lax.ppermute(rows_for(block, jnp.logical_not(low_side), 2), "space", even)
        odd_v = swap_odd(rows_for(block, low_side, 2))
        wide = widened(block, even_v, odd_v)[0]
        wide = jnp.where(inside, update(wide, coefs[0, 1:-1], coefs[1, 1:-1]), 0.0)
        return update(wide, coarse[1], coarse[2])

    slice_id = lax.axis_index("tm")
    slices = lax.axis_size("tm")
    onward = [(i, i + 1) for i in range(slices - 1)]

    def link(position, state):
        incoming = lax.ppermute(state, "tm", onward)
        return jnp.where(slice_id > 0, advance(incoming), 0.0) + jump

    return lax.fori_loop(0, slices - 1, link, jump)


def per_device(starts, diffusivity, reaction):
    height, breadth = starts.shape[2:]
    small = height // 4
    slices = lax.axis_size("tm")
    behind = slices - 1
    reach = COARSE * behind
    at_once = 0 < behind and reach <= small
    even = even_pairs()
    low_side = parity() == 0
    high_side = jnp.logical_not(low_side)

    odd_rows = odd_pack(starts, diffusivity, reaction)
    odd_got = swap_odd(odd_rows)
    even_rows, even_rest = even_pack(odd_rows, starts, diffusivity, reaction)
    even_got = lax.ppermute(even_rows, "space", even)
    even_got_rest = lax.ppermute(even_rest, "space", even)
    fine, low_steps, high_steps, coarse, end = inner(starts, diffusivity, reaction)
    mended, end, odd_outer = even_edge(starts, diffusivity, reaction, low_steps, high_steps, even_got, end)
    rows, end, jump = edge(odd_outer, low_steps, high_steps, odd_got, even_got_rest, end, coarse)
    width = reach if at_once else COARSE
    later, jump = lax.optimization_barrier((coarse[1:], jump))
    odd_c = swap_odd(rows_for(later, low_side, width))
    even_c = lax.ppermute(rows_for(later, high_side, width), "space", even)
    if at_once:
        before = [
            lax.ppermute(jump, "tm", [(i, (i + k) % slices) for i in range(slices)])
            for k in range(behind, 0, -1)
        ]

        def halo(low):
            return jnp.concatenate(
                [rows_for(before[j][None], low, reach - COARSE * j)[0] for j in range(behind)], axis=0
            )

        odd_j = swap_odd(halo(low_side))
        even_j = lax.ppermute(halo(high_side), "space", even)
        return last(before, even_j, odd_j, *ready(fine, rows, mended, end, jump, coarse, even_c, odd_c))
    chained = relay(jump, coarse, even_c, odd_c, even)
    change = jnp.repeat(jnp.repeat(jnp.transpose(chained - end, (1, 0, 2)), 4, axis=1), 4, axis=2)
    fixed = jnp.where(low_side, 0, height - 4)
    fine = jnp.transpose(fine, (0, 2, 1, 3)).reshape(8, height, breadth)
    fine = lax.dynamic_update_slice_in_dim(fine, jnp.transpose(rows, (1, 0, 2)), fixed, axis=1)
    fine = lax.dynamic_update_slice_in_dim(fine, jnp.transpose(mended, (1, 0, 2)), height - 4 - fixed, axis=1)
    return (fine + change)[None]


def solution(mesh):
    in_specs = (P("tm", None, "space", None), P(None, "space", None), P(None, "space", None))
    out_specs = P("tm", None, "space", None)
    return jax.shard_map(per_device, mesh=mesh, in_specs=in_specs, out_specs=out_specs, check_vma=False)
```
